512 devices in a mesh: expert: 64 (over x, z), shard: 8 (over y, core).
Axes of the slice: x: 4, y: 4, z: 16, core: 2. Of those that a mesh axis runs over, the one named last changes fastest.
Arguments:
- tokens: bfloat16 [8192, 4096], P('expert'), may hold values from -6 to 6
- slot_lists: int32 [64, 64, 8], P(None, 'expert'), may hold values from -1 to 127, as said below
- slot_gates: float32 [64, 64, 8], P(None, 'expert'), may hold values from 0.1 to 1
- counts: int32 [8192], P('expert'), may hold values from 0 to 64, as said below
- gate_weight: bfloat16 [64, 4096, 1024], P('expert', None, 'shard'), may hold values from -0.09375 to 0.09375
- up_weight: bfloat16 [64, 4096, 1024], P('expert', None, 'shard'), may hold values from -0.09375 to 0.09375
- down_weight: bfloat16 [64, 1024, 4096], P('expert', 'shard'), may hold values from -0.1875 to 0.1875
Outputs:
- combined: bfloat16 [8192, 4096], P('expert', 'shard')
The draws below stay inside these ranges and needn't reach their ends.
Inputs may be any that keep to these rules, and one draw needn't show every extreme that they name: Each block slot_lists[e, o] names distinct tokens of owner o in its leading entries, one or more, and holds -1 after them; in every draw one expert's blocks are full from every owner, and every expert names token 0 of owner 0. counts[t] is the number of live slots, over all experts, that name token t.
All inputs are finite; a program needn't handle non-finite values.
Results may differ from the reference program's by a relative error of at most 0.019.
Values may be sent and summed in bfloat16 or wider, within the bound.
No kernel may reach another device: no remote copies, remote signals or barrier semaphores. Data moves between devices by JAX's collectives and lax.ppermute only.
A program may use at most 64 MiB of HBM per device.

```python
import math
import jax
import jax.numpy as jnp
from jax import lax

D = 4096
H = 1024
TOK_DEV = 128
SLOT = 8
EXPERTS = 64
TOKENS = 8192
CAP = 512
HS = 128
N_EXPERT = 64
N_SHARD = 8


def choose_slots(key):
    key = jax.random.fold_in(key, 11)
    key_scores, key_levels, key_fill, key_full = jax.random.split(key, 4)
    positions = jnp.arange(TOK_DEV, dtype=jnp.int32)
    scores = jax.random.randint(key_scores, (EXPERTS, N_EXPERT, TOK_DEV), 0, 2 ** 19, dtype=jnp.int32) * TOK_DEV + positions
    owner_ids = jnp.arange(N_EXPERT, dtype=jnp.int32)[None, :, None]
    forced = jnp.logical_and(owner_ids == 0, positions[None, None, :] == 0)
    scores = jnp.where(forced, jnp.int32(2 ** 31 - 1), scores)
    _, chosen = lax.top_k(scores, SLOT)
    levels = jax.random.randint(key_levels, (EXPERTS, 1), 1, 5, dtype=jnp.int32)
    ceiling = jnp.maximum(SLOT * levels // 4, 1)
    lowest = jnp.maximum(ceiling // 2, 1)
    fill_counts = jax.random.randint(key_fill, (EXPERTS, N_EXPERT), lowest, ceiling + 1, dtype=jnp.int32)
    full_expert = jax.random.randint(key_full, (), 0, EXPERTS, dtype=jnp.int32)
    expert_ids = jnp.arange(EXPERTS, dtype=jnp.int32)[:, None]
    fill_counts = jnp.where(expert_ids == full_expert, SLOT, fill_counts)
    slot_index = jnp.arange(SLOT, dtype=jnp.int32)
    return jnp.where(slot_index < fill_counts[:, :, None], chosen.astype(jnp.int32), -1).astype(jnp.int32)


def draw_slot_lists(key, part):
    return choose_slots(key)


def draw_counts(key, part):
    slot_table = choose_slots(key)
    usable = slot_table >= 0
    owner_base = (jnp.arange(N_EXPERT, dtype=jnp.int32) * TOK_DEV)[None, :, None]
    targets = jnp.where(usable, slot_table + owner_base, TOKENS).reshape(-1)
    ones_column = jnp.ones(targets.shape, jnp.int32)
    return jax.ops.segment_sum(ones_column, targets, num_segments=TOKENS + 1)[:TOKENS].astype(jnp.int32)


def block_levels(stream_key, dims, pieces, least, largest):
    factor_of = 1.0
    for position, blocks in pieces:
        heights = jax.random.uniform(jax.random.fold_in(jax.random.fold_in(stream_key, 6), position), (blocks,), jnp.float32, least / len(pieces), largest / len(pieces))
        factor_of = factor_of * jnp.repeat(jnp.exp(heights), dims[position] // blocks).reshape((-1,) + (1,) * (len(dims) - 1 - position))
    return factor_of


def centred(own_key, shape, spread, reach, cuts=(), kind=jnp.bfloat16):
    drawn = spread * jax.random.normal(own_key, shape, jnp.float32)
    if cuts:
        drawn = drawn * block_levels(own_key, shape, cuts, -0.22, 0.18)
    return jnp.clip(drawn, -reach, reach).astype(kind)


def setup_inputs(seed: int = 0) -> dict:
    seeds = jax.random.split(jax.random.key(seed), 8)
    tokens = centred(seeds[0], (TOKENS, D), 1.0, 6.0, ((0, 64),))
    slot_lists = draw_slot_lists(jax.random.fold_in(seeds[7], 71), 0)
    slot_gates = jnp.clip(jnp.exp(math.log(1.0) - 2.3025851 * jax.random.uniform(seeds[2], (EXPERTS, N_EXPERT, SLOT), jnp.float32) ** block_levels(seeds[2], (EXPERTS, N_EXPERT, SLOT), ((1, 64),), -0.2, 0.2)), 0.1, 1.0)
    counts = draw_counts(jax.random.fold_in(seeds[7], 71), 0)
    gate_weight = centred(seeds[4], (EXPERTS, D, H), D ** -0.5, 0.09375, ((0, 64), (2, 8)))
    up_weight = centred(seeds[5], (EXPERTS, D, H), D ** -0.5, 0.09375, ((0, 64), (2, 8)))
    down_weight = centred(seeds[6], (EXPERTS, H, D), H ** -0.5, 0.1875, ((0, 64), (1, 8)))
    return {"tokens": tokens, "slot_lists": slot_lists, "slot_gates": slot_gates, "counts": counts, "gate_weight": gate_weight, "up_weight": up_weight, "down_weight": down_weight}


def reference(tokens, slot_lists, slot_gates, counts, gate_weight, up_weight, down_weight):
    owner_base = (jnp.arange(N_EXPERT, dtype=jnp.int32) * TOK_DEV)[:, None]

    def expert_step(totals, expert_id):
        entries = lax.dynamic_index_in_dim(slot_lists, expert_id, 0, keepdims=False)
        gates_here = lax.dynamic_index_in_dim(slot_gates, expert_id, 0, keepdims=False)
        usable = entries >= 0
        row_ids = jnp.where(usable, entries + owner_base, 0).reshape(-1).astype(jnp.int32)
        picked = jnp.take(tokens, row_ids, axis=0)
        gathered = jnp.where(usable.reshape(-1, 1), picked, jnp.zeros_like(picked)).astype(jnp.bfloat16)
        gate_rows = lax.dynamic_index_in_dim(gate_weight, expert_id, 0, keepdims=False)
        up_rows = lax.dynamic_index_in_dim(up_weight, expert_id, 0, keepdims=False)
        down_rows = lax.dynamic_index_in_dim(down_weight, expert_id, 0, keepdims=False)
        gate_act = jnp.dot(gathered, gate_rows, preferred_element_type=jnp.float32)
        up_act = jnp.dot(gathered, up_rows, preferred_element_type=jnp.float32)
        hidden = (jax.nn.silu(gate_act) * up_act).astype(jnp.bfloat16)
        hidden_split = hidden.reshape(CAP, N_SHARD, HS).astype(jnp.float32)
        down_split = down_rows.reshape(N_SHARD, HS, D).astype(jnp.float32)
        partials = jnp.einsum("csh,shd->scd", hidden_split, down_split, precision=lax.Precision.HIGHEST)
        rounded = lax.optimization_barrier(partials.astype(jnp.bfloat16))
        outputs = jnp.sum(rounded.astype(jnp.float32), axis=0).astype(jnp.bfloat16)
        gate_values = jnp.where(usable, gates_here, jnp.zeros_like(gates_here)).reshape(-1)
        weighted = outputs.astype(jnp.float32) * gate_values[:, None]
        targets = jnp.where(usable, entries + owner_base, TOKENS).reshape(-1).astype(jnp.int32)
        added = jax.ops.segment_sum(weighted, targets, num_segments=TOKENS + 1)[:TOKENS]
        return totals + added, None

    start_totals = jnp.zeros((TOKENS, D), jnp.float32)
    totals, _ = lax.scan(expert_step, start_totals, jnp.arange(EXPERTS, dtype=jnp.int32))
    divisor = jnp.maximum(counts.astype(jnp.float32), 1.0)
    return (totals / divisor[:, None]).astype(jnp.bfloat16)
```

```python
import jax
import jax.numpy as jnp
import numpy as np
from jax import lax
from jax.sharding import Mesh, PartitionSpec as P

E = ("x", "z")
S = ("y", "core")
NY = 4
BF = jnp.bfloat16
F32 = jnp.float32


def dot(a, b):
    return jnp.dot(a, b, preferred_element_type=F32)


def swap_cores(a):
    return lax.ppermute(a, "core", [(0, 1), (1, 0)])


def local(tokens, slot_lists, slot_gates, counts, gate_weight, up_weight, down_weight):
    y = lax.axis_index("y")
    c = lax.axis_index("core")
    width = tokens.shape[1] // (2 * NY)
    group = 2 * width
    rows = slot_lists.shape[0] * slot_lists.shape[2]
    local_tokens = tokens.shape[0]
    gate_weight, up_weight, down_weight = gate_weight[0], up_weight[0], down_weight[0]

    own = lax.dynamic_slice_in_dim(tokens, (y * 2 + c) * width, width, 1)
    flat = slot_lists.reshape(rows, 1)
    onehot = (flat == lax.broadcasted_iota(jnp.int32, (rows, local_tokens), 1)).astype(BF)
    picked = dot(onehot, own).astype(BF)
    arrived = lax.all_to_all(picked.reshape(-1, 8, width), E, 0, 0, tiled=True).reshape(rows, width)

    gu, dn = [], []
    for d in range(NY):
        to = (y + d) % NY
        g = lax.dynamic_slice_in_dim(gate_weight, to * group, group, 0)
        u = lax.dynamic_slice_in_dim(up_weight, to * group, group, 0)
        w = jnp.concatenate([g, u], axis=1)
        v = lax.dynamic_slice_in_dim(down_weight, to * group, group, 1)
        if d:
            ring = [(j, (j + d) % NY) for j in range(NY)]
            w = lax.ppermute(w, "y", ring)
            v = lax.ppermute(v, "y", ring)
        gu.append(w)
        dn.append(v)

    arrived, gu, dn = lax.optimization_barrier((arrived, gu, dn))
    other = swap_cores(arrived)
    parts = []
    for d in range(NY):
        w_own = lax.dynamic_slice_in_dim(gu[d], c * width, width, 0)
        w_other = lax.dynamic_slice_in_dim(gu[d], (1 - c) * width, width, 0)
        parts.append((dot(arrived, w_own) + dot(other, w_other)).astype(BF))
    ordered = jnp.stack([parts[(NY - k) % NY] for k in range(NY)] * 2)
    ordered = lax.dynamic_slice_in_dim(ordered, NY - y, NY, 0)
    sums = lax.all_to_all(ordered, "y", 0, 0, tiled=True).astype(F32).sum(0)
    half = sums.shape[1] // 2
    hidden = (jax.nn.silu(sums[:, :half]) * sums[:, half:]).astype(BF)
    gathered = lax.all_to_all(jnp.broadcast_to(hidden, (NY,) + hidden.shape), "y", 0, 0, tiled=True)
    out = 0.0
    for d in range(NY):
        h = lax.dynamic_index_in_dim(gathered, (y - d) % NY, 0, keepdims=False)
        out = out + dot(h, dn[d])
    keep = lax.dynamic_slice_in_dim(out, c * width, width, 1)
    give = lax.dynamic_slice_in_dim(out, (1 - c) * width, width, 1).astype(BF)
    result = (keep + swap_cores(give).astype(F32)).astype(BF)
    returned = lax.all_to_all(result.reshape(-1, 8, width), E, 0, 0, tiled=True).reshape(rows, width)

    hit = slot_lists.reshape(1, rows) == lax.broadcasted_iota(jnp.int32, (local_tokens, rows), 0)
    weight = jnp.where(hit, slot_gates.reshape(1, rows), 0.0)
    totals = 0.0
    for _ in range(3):
        piece = weight.astype(BF)
        weight = weight - piece.astype(F32)
        totals = totals + dot(piece, returned)
    divisor = jnp.maximum(counts.astype(F32), 1.0)
    return (totals / divisor[:, None]).astype(BF)


def solution(mesh):
    fine = Mesh(np.asarray(mesh.devices).reshape(4, 16, NY, 2), ("x", "z", "y", "core"))
    return jax.shard_map(
        local,
        mesh=fine,
        in_specs=(
            P(E, None),
            P(None, E, None),
            P(None, E, None),
            P(E),
            P(E, None, S),
            P(E, None, S),
            P(E, S, None),
        ),
        out_specs=P(E, S),
        check_vma=False,
    )
```

```python
import functools

import jax
import jax.numpy as jnp
import numpy as np
from jax import lax
from jax.experimental import pallas as pl
from jax.experimental.pallas import tpu as pltpu
from jax.sharding import Mesh, PartitionSpec as P

E = ("x", "z")
S = ("y", "core")
NY = 4
HS = 128
BF = jnp.bfloat16
F32 = jnp.float32
HINT = 60 * 10**9
VMEM_LIMIT = 32 * 1024 * 1024
WHOLE = 60 * 1024 * 1024

SMEM = pl.BlockSpec(memory_space=pltpu.SMEM)
VMEM = pl.BlockSpec(memory_space=pltpu.VMEM)
ANY = pl.BlockSpec(memory_space=pl.ANY)


def dot(a, b):
    return jnp.dot(a, b, preferred_element_type=F32)


def call(kernel, out_shape, in_specs, out_specs, flops=0, bytes_accessed=1 << 20, vmem=VMEM_LIMIT, **more):
    return pl.pallas_call(
        kernel,
        out_shape=out_shape,
        in_specs=in_specs,
        out_specs=out_specs,
        compiler_params=pltpu.CompilerParams(vmem_limit_bytes=vmem),
        cost_estimate=pl.CostEstimate(flops=flops, bytes_accessed=bytes_accessed, transcendentals=0),
        **more,
    )


def swap_cores(a):
    return lax.ppermute(a, "core", [(0, 1), (1, 0)])


def block_copies(to, gate, up, down, out, sems):
    group = out.shape[1]
    first = pl.multiple_of(to * group, group)
    copies = [
        pltpu.make_async_copy(gate.at[pl.ds(first, group)], out.at[0], sems.at[0]),
        pltpu.make_async_copy(up.at[pl.ds(first, group)], out.at[1], sems.at[1]),
    ]
    for j in range(group // HS):
        column = pl.multiple_of(first + j * HS, HS)
        copies.append(
            pltpu.make_async_copy(
                down.at[:, pl.ds(column, HS)], out.at[2, pl.ds(j * HS, HS)], sems.at[2 + j]
            )
        )
    return copies


def spread(values, rows):
    slots, experts = values.shape
    lane = lax.broadcasted_iota(jnp.int32, (experts, rows), 1)
    expert = lax.broadcasted_iota(jnp.int32, (experts, rows), 0)
    wide = dot(values.astype(BF), (lane // slots == expert).astype(BF))
    lane = lax.broadcasted_iota(jnp.int32, (slots, rows), 1)
    slot = lax.broadcasted_iota(jnp.int32, (slots, rows), 0)
    return jnp.sum(jnp.where(lane % slots == slot, wide, 0.0), axis=0, keepdims=True)


def start_kernel(at, slots, tokens, gate, up, down, picked, b1, b2, b3, own, sems, own_sem):
    width = own.shape[1]
    local_tokens = tokens.shape[0]
    first = pl.multiple_of((at[0] * 2 + at[1]) * width, width)
    fetch = pltpu.make_async_copy(tokens.at[:, pl.ds(first, width)], own, own_sem)
    fetch.start()
    copies = []
    for d, out in ((2, b2), (1, b1), (3, b3)):
        copies += block_copies(lax.rem(at[0] + d, NY), gate, up, down, out, sems.at[d - 1])
    for copy in copies:
        copy.start()
    rows = picked.shape[0]
    names = spread(slots[...].astype(F32), rows)
    token = lax.broadcasted_iota(jnp.int32, (local_tokens, rows), 0).astype(F32)
    hit = (names == token).astype(BF)
    fetch.wait()
    picked[...] = lax.dot_general(
        hit, own[...], (((0,), (0,)), ((), ())), preferred_element_type=F32
    ).astype(BF)
    for copy in copies:
        copy.wait()


def start(at, slots, tokens, gate, up, down):
    group = gate.shape[0] // NY
    width = tokens.shape[1] // (2 * NY)
    rows = slots.shape[0] * slots.shape[1]
    block = jax.ShapeDtypeStruct((3, group, HS), BF)
    return call(
        start_kernel,
        (jax.ShapeDtypeStruct((rows, width), BF), block, block, block),
        [SMEM, VMEM, ANY, ANY, ANY, ANY],
        (VMEM, VMEM, VMEM, VMEM),
        bytes_accessed=5 << 20,
        vmem=WHOLE,
        scratch_shapes=[
            pltpu.VMEM((tokens.shape[0], width), BF),
            pltpu.SemaphoreType.DMA((NY - 1, 2 + group // HS)),
            pltpu.SemaphoreType.DMA,
        ],
    )(at, slots, tokens, gate, up, down)


def own_block_kernel(at, gate, up, down, out, sems):
    copies = block_copies(at[0], gate, up, down, out, sems)
    for copy in copies:
        copy.start()
    for copy in copies:
        copy.wait()


def own_block(at, gate, up, down):
    group = gate.shape[0] // NY
    return call(
        own_block_kernel,
        jax.ShapeDtypeStruct((3, group, HS), BF),
        [SMEM, ANY, ANY, ANY],
        VMEM,
        vmem=WHOLE,
        scratch_shapes=[pltpu.SemaphoreType.DMA((2 + group // HS,))],
    )(at, gate, up, down)


def ready_kernel(first, second, out, sem):
    copy = pltpu.make_async_copy(first.at[0, pl.ds(0, out.shape[0])], out, sem)
    copy.start()
    copy.wait()


def ready(first, second):
    return call(
        ready_kernel,
        jax.ShapeDtypeStruct((16, HS), BF),
        [ANY, ANY],
        VMEM,
        flops=HINT,
        scratch_shapes=[pltpu.SemaphoreType.DMA],
    )(first, second)


def partial_kernel(distances, at, own, other, *refs):
    blocks, out = refs[: len(distances)], refs[-1]
    rows, width = own.shape
    step = 256
    mine = pl.multiple_of(at[1] * width, width)
    theirs = pl.multiple_of((1 - at[1]) * width, width)
    for d, w in zip(distances, blocks):
        owner = lax.rem(at[0] + NY - d, NY)
        a = jnp.concatenate([w[0, pl.ds(mine, width)], w[1, pl.ds(mine, width)]], axis=1)
        b = jnp.concatenate([w[0, pl.ds(theirs, width)], w[1, pl.ds(theirs, width)]], axis=1)
        for r in range(0, rows, step):
            total = dot(own[pl.ds(r, step)], a) + dot(other[pl.ds(r, step)], b)
            out[owner, pl.ds(r, step)] = total.astype(BF)


def partial_sums(at, own, other, blocks, distances, last):
    rows, width = own.shape
    operands = [at, own, other] + [blocks[d] for d in distances]
    specs = [SMEM] + [VMEM] * (len(operands) - 1)
    more = {}
    if last[0].shape == (NY, rows, 2 * HS):
        more = {"input_output_aliases": {len(operands): 0}}
    operands += last
    specs.append(VMEM)
    return call(
        functools.partial(partial_kernel, distances),
        jax.ShapeDtypeStruct((NY, rows, 2 * HS), BF),
        specs,
        VMEM,
        flops=2 * rows * 2 * width * len(distances) * 2 * HS,
        **more,
    )(*operands)


def hidden_kernel(sums, out):
    total = sums[0].astype(F32)
    for k in range(1, NY):
        total = total + sums[k].astype(F32)
    gate, up = total[:, :HS], total[:, HS:]
    hidden = (gate / (1.0 + jnp.exp(-gate)) * up).astype(BF)
    for k in range(NY):
        out[k] = hidden


def hidden_copies(sums):
    return call(
        hidden_kernel, jax.ShapeDtypeStruct((NY, sums.shape[1], HS), BF), [VMEM], VMEM
    )(sums)


def out_kernel(mine, at, hidden, w0, w1, w2, w3, out):
    rows = hidden.shape[1]
    width = out.shape[1]
    step = 256
    first = (at[1] if mine else 1 - at[1]) * width
    owners = [lax.rem(at[0] + NY - d, NY) for d in range(NY)]
    for j in range(0, width, 2 * HS):
        one = pl.multiple_of(first + j, HS)
        two = pl.multiple_of(first + j + HS, HS)
        b = jnp.concatenate(
            [
                jnp.concatenate([w[2, pl.ds(one, HS)], w[2, pl.ds(two, HS)]], axis=1)
                for w in (w0, w1, w2, w3)
            ],
            axis=0,
        )
        for r in range(0, rows, step):
            a = jnp.concatenate([hidden[k, pl.ds(r, step)] for k in owners], axis=1)
            out[pl.ds(r, step), pl.ds(j, 2 * HS)] = dot(a, b).astype(out.dtype)


def out_sums(at, hidden, blocks, width, mine):
    rows = hidden.shape[1]
    return call(
        functools.partial(out_kernel, mine),
        jax.ShapeDtypeStruct((rows, width), F32 if mine else BF),
        [SMEM] + [VMEM] * 5,
        VMEM,
        flops=2 * rows * width * NY * HS,
    )(at, hidden, *blocks)


def local(tokens, slot_lists, slot_gates, counts, gate_weight, up_weight, down_weight):
    y = lax.axis_index("y")
    c = lax.axis_index("core")
    at = jnp.stack([y, c]).astype(jnp.int32)
    width = tokens.shape[1] // (2 * NY)
    rows = slot_lists.shape[0] * slot_lists.shape[2]
    local_tokens = tokens.shape[0]
    gate_weight, up_weight, down_weight = gate_weight[0], up_weight[0], down_weight[0]

    slots = slot_lists.transpose(2, 1, 0).reshape(slot_lists.shape[2], slot_lists.shape[0])
    picked, *sent = start(at, slots, tokens, gate_weight, up_weight, down_weight)
    arrived = lax.all_to_all(picked.reshape(-1, 8, width), E, 0, 0, tiled=True).reshape(rows, width)
    blocks = [own_block(at, gate_weight, up_weight, down_weight)]
    for d in range(1, NY):
        blocks.append(lax.ppermute(sent[d - 1], "y", [(j, (j + d) % NY) for j in range(NY)]))
    arrived, early = lax.optimization_barrier((arrived, ready(blocks[0], blocks[2])))
    other = swap_cores(arrived)
    parts = partial_sums(at, arrived, other, blocks, (0, 2, 1), (early,))
    parts = partial_sums(at, arrived, other, blocks, (3,), (parts,))
    sums = lax.all_to_all(parts, "y", 0, 0, tiled=True)
    gathered = lax.all_to_all(hidden_copies(sums), "y", 0, 0, tiled=True)
    give = swap_cores(out_sums(at, gathered, blocks, width, False))
    keep = out_sums(at, gathered, blocks, width, True)
    result = (keep + give.astype(F32)).astype(BF)
    returned = lax.all_to_all(result.reshape(-1, 8, width), E, 0, 0, tiled=True).reshape(rows, width)

    hit = slot_lists.reshape(1, rows) == lax.broadcasted_iota(jnp.int32, (local_tokens, rows), 0)
    weight = jnp.where(hit, slot_gates.reshape(1, rows), 0.0)
    totals = 0.0
    for _ in range(3):
        piece = weight.astype(BF)
        weight = weight - piece.astype(F32)
        totals = totals + dot(piece, returned)
    divisor = jnp.maximum(counts.astype(F32), 1.0)
    return (totals / divisor[:, None]).astype(BF)


def solution(mesh):
    fine = Mesh(np.asarray(mesh.devices).reshape(4, 16, NY, 2), ("x", "z", "y", "core"))
    return jax.shard_map(
        local,
        mesh=fine,
        in_specs=(
            P(E, None),
            P(None, E, None),
            P(None, E, None),
            P(E),
            P(E, None, S),
            P(E, None, S),
            P(E, S, None),
        ),
        out_specs=P(E, S),
        check_vma=False,
    )
```

```python
import functools

import jax
import jax.numpy as jnp
import numpy as np
from jax import lax
from jax.experimental import pallas as pl
from jax.experimental.pallas import tpu as pltpu
from jax.sharding import Mesh, PartitionSpec as P

E = ("x", "z")
S = ("y", "core")
NY = 4
HS = 128
BF = jnp.bfloat16
F32 = jnp.float32
HINT = 60 * 10**9
VMEM_LIMIT = 32 * 1024 * 1024
WHOLE = 60 * 1024 * 1024

SMEM = pl.BlockSpec(memory_space=pltpu.SMEM)
VMEM = pl.BlockSpec(memory_space=pltpu.VMEM)
ANY = pl.BlockSpec(memory_space=pl.ANY)


def dot(a, b):
    return jnp.dot(a, b, preferred_element_type=F32)


def call(kernel, out_shape, in_specs, out_specs, flops=0, bytes_accessed=1 << 20, vmem=VMEM_LIMIT, **more):
    return pl.pallas_call(
        kernel,
        out_shape=out_shape,
        in_specs=in_specs,
        out_specs=out_specs,
        compiler_params=pltpu.CompilerParams(vmem_limit_bytes=vmem),
        cost_estimate=pl.CostEstimate(flops=flops, bytes_accessed=bytes_accessed, transcendentals=0),
        **more,
    )


def swap_cores(a):
    return lax.ppermute(a, "core", [(0, 1), (1, 0)])


def block_copies(to, gate, up, down, out, sems):
    group = out.shape[1]
    first = pl.multiple_of(to * group, group)
    copies = [
        pltpu.make_async_copy(gate.at[pl.ds(first, group)], out.at[0], sems.at[0]),
        pltpu.make_async_copy(up.at[pl.ds(first, group)], out.at[1], sems.at[1]),
    ]
    for j in range(group // HS):
        column = pl.multiple_of(first + j * HS, HS)
        copies.append(
            pltpu.make_async_copy(
                down.at[:, pl.ds(column, HS)], out.at[2, pl.ds(j * HS, HS)], sems.at[2 + j]
            )
        )
    return copies


def spread(values, rows):
    slots, experts = values.shape
    lane = lax.broadcasted_iota(jnp.int32, (experts, rows), 1)
    expert = lax.broadcasted_iota(jnp.int32, (experts, rows), 0)
    wide = dot(values.astype(BF), (lane // slots == expert).astype(BF))
    lane = lax.broadcasted_iota(jnp.int32, (slots, rows), 1)
    slot = lax.broadcasted_iota(jnp.int32, (slots, rows), 0)
    return jnp.sum(jnp.where(lane % slots == slot, wide, 0.0), axis=0, keepdims=True)


def position():
    return lax.axis_index("y"), lax.axis_index("core")


def start_kernel(far, slots, tokens, gate, up, down, picked, block, own, rows_out, held, sems, own_sem, out_sems):
    y, c = position()
    width = own.shape[1]
    local_tokens = tokens.shape[0]
    first = pl.multiple_of((y * 2 + c) * width, width)
    fetch = pltpu.make_async_copy(tokens.at[:, pl.ds(first, width)], own, own_sem)
    fetch.start()
    copies = block_copies(lax.rem(y + far, NY), gate, up, down, held, sems)
    for copy in copies:
        copy.start()
    rows = picked.shape[0]
    names = spread(slots[...].astype(F32), rows)
    token = lax.broadcasted_iota(jnp.int32, (local_tokens, rows), 0).astype(F32)
    hit = (names == token).astype(BF)
    fetch.wait()
    for copy in copies:
        copy.wait()
    send = pltpu.make_async_copy(held, block, out_sems.at[0])
    send.start()
    sends = [send]
    step = rows // 2
    for n in range(2):
        part = pl.ds(n * step, step)
        rows_out[part] = lax.dot_general(
            hit[:, n * step : (n + 1) * step], own[...], (((0,), (0,)), ((), ())), preferred_element_type=F32
        ).astype(BF)
        send = pltpu.make_async_copy(rows_out.at[part], picked.at[part], out_sems.at[1 + n])
        send.start()
        sends.append(send)
    for send in sends:
        send.wait()


def start(far, slots, tokens, gate, up, down):
    group = gate.shape[0] // NY
    width = tokens.shape[1] // (2 * NY)
    rows = slots.shape[0] * slots.shape[1]
    return call(
        functools.partial(start_kernel, far),
        (jax.ShapeDtypeStruct((rows, width), BF), jax.ShapeDtypeStruct((3, group, HS), BF)),
        [VMEM, ANY, ANY, ANY, ANY],
        (ANY, ANY),
        bytes_accessed=5 << 20,
        vmem=WHOLE,
        scratch_shapes=[
            pltpu.VMEM((tokens.shape[0], width), BF),
            pltpu.VMEM((rows, width), BF),
            pltpu.VMEM((3, group, HS), BF),
            pltpu.SemaphoreType.DMA((2 + group // HS,)),
            pltpu.SemaphoreType.DMA,
            pltpu.SemaphoreType.DMA((3,)),
        ],
    )(slots, tokens, gate, up, down)


def pack_kernel(d, gate, up, down, out, sems):
    copies = block_copies(lax.rem(position()[0] + d, NY), gate, up, down, out, sems)
    for copy in copies:
        copy.start()
    for copy in copies:
        copy.wait()


def pack(d, gate, up, down):
    group = gate.shape[0] // NY
    return call(
        functools.partial(pack_kernel, d),
        jax.ShapeDtypeStruct((3, group, HS), BF),
        [ANY, ANY, ANY],
        VMEM,
        vmem=WHOLE,
        scratch_shapes=[pltpu.SemaphoreType.DMA((2 + group // HS,))],
    )(gate, up, down)


def ready_kernel(first, second, out, sem):
    copy = pltpu.make_async_copy(first.at[0, pl.ds(0, out.shape[0])], out, sem)
    copy.start()
    copy.wait()


def ready(first, second):
    return call(
        ready_kernel,
        jax.ShapeDtypeStruct((16, HS), BF),
        [ANY, ANY],
        VMEM,
        flops=HINT,
        scratch_shapes=[pltpu.SemaphoreType.DMA],
    )(first, second)


def partial_kernel(own_ref, other, w0, w1, w2, w3, early, out, own, sem):
    fetch = pltpu.make_async_copy(own_ref, own, sem)
    fetch.start()
    y, c = position()
    rows, width = own.shape
    step = 256
    mine = pl.multiple_of(c * width, width)
    theirs = pl.multiple_of((1 - c) * width, width)
    for d, w in enumerate((w0, w1, w2, w3)):
        owner = lax.rem(y + NY - d, NY)
        b = jnp.concatenate([w[0, pl.ds(theirs, width)], w[1, pl.ds(theirs, width)]], axis=1)
        a = jnp.concatenate([w[0, pl.ds(mine, width)], w[1, pl.ds(mine, width)]], axis=1)
        for r in range(0, rows, step):
            total = dot(other[pl.ds(r, step)], b)
            if d == 0 and r == 0:
                fetch.wait()
            total = total + dot(own[pl.ds(r, step)], a)
            out[owner, pl.ds(r, step)] = total.astype(BF)


def partial_sums(own, other, blocks, early):
    rows, width = own.shape
    return call(
        partial_kernel,
        jax.ShapeDtypeStruct((NY, rows, 2 * HS), BF),
        [ANY] + [VMEM] * 5 + [ANY],
        VMEM,
        flops=2 * rows * 2 * width * NY * 2 * HS,
        scratch_shapes=[pltpu.VMEM((rows, width), BF), pltpu.SemaphoreType.DMA],
    )(own, other, *blocks, early)


def hidden_kernel(sums, out):
    total = sums[0].astype(F32)
    for k in range(1, NY):
        total = total + sums[k].astype(F32)
    gate, up = total[:, :HS], total[:, HS:]
    hidden = (gate / (1.0 + jnp.exp(-gate)) * up).astype(BF)
    for k in range(NY):
        out[k] = hidden


def hidden_copies(sums):
    return call(
        hidden_kernel, jax.ShapeDtypeStruct((NY, sums.shape[1], HS), BF), [VMEM], VMEM
    )(sums)


def out_kernel(mine, hidden, w0, w1, w2, w3, out):
    y, c = position()
    rows = hidden.shape[1]
    width = out.shape[1]
    first = (c if mine else 1 - c) * width
    owners = [lax.rem(y + NY - d, NY) for d in range(NY)]
    a = jnp.concatenate([hidden[k] for k in owners], axis=1)
    for j in range(0, width, 2 * HS):
        one = pl.multiple_of(first + j, HS)
        two = pl.multiple_of(first + j + HS, HS)
        b = jnp.concatenate(
            [
                jnp.concatenate([w[2, pl.ds(one, HS)], w[2, pl.ds(two, HS)]], axis=1)
                for w in (w0, w1, w2, w3)
            ],
            axis=0,
        )
        out[:, pl.ds(j, 2 * HS)] = dot(a, b).astype(out.dtype)


def out_sums(hidden, blocks, width, mine):
    rows = hidden.shape[1]
    return call(
        functools.partial(out_kernel, mine),
        jax.ShapeDtypeStruct((rows, width), F32 if mine else BF),
        [VMEM] * 5,
        VMEM,
        flops=2 * rows * width * NY * HS,
    )(hidden, *blocks)


def weight_kernel(slots, gates, out):
    tokens, rows = out.shape[1:]
    names = spread(slots[...].astype(F32), rows)
    hit = names == lax.broadcasted_iota(jnp.int32, (tokens, rows), 0).astype(F32)
    left = gates[...]
    for p in range(out.shape[0]):
        piece = left.astype(BF).astype(F32)
        left = left - piece
        out[p] = jnp.where(hit, spread(piece, rows), 0.0).astype(BF)


def token_weights(slots, gates, tokens):
    rows = slots.shape[0] * slots.shape[1]
    return call(
        weight_kernel, jax.ShapeDtypeStruct((3, tokens, rows), BF), [VMEM, VMEM], VMEM
    )(slots, gates)


def finish_kernel(weights, returned, counts, out):
    divisor = jnp.maximum(counts[...].astype(F32), 1.0)
    rows = returned[...]
    total = dot(weights[2], rows) + dot(weights[1], rows)
    total = total + dot(weights[0], rows)
    out[...] = (total / divisor).astype(BF)


def finish(weights, returned, counts):
    return call(
        finish_kernel,
        jax.ShapeDtypeStruct((weights.shape[1], returned.shape[1]), BF),
        [VMEM] * 3,
        VMEM,
    )(weights, returned, counts)


def local(tokens, slot_lists, slot_gates, counts, gate_weight, up_weight, down_weight):
    width = tokens.shape[1] // (2 * NY)
    experts, _, slots = slot_lists.shape
    rows = experts * slots
    weights = gate_weight[0], up_weight[0], down_weight[0]
    names = slot_lists.transpose(2, 1, 0).reshape(slots, experts)
    gates = slot_gates.transpose(2, 1, 0).reshape(slots, experts)

    far = 2
    picked, first = start(far, names, tokens, *weights)
    blocks = []
    for d in range(NY):
        block = first if d == far else pack(d, *weights)
        blocks.append(lax.ppermute(block, "y", [(j, (j + d) % NY) for j in range(NY)]) if d else block)
    arrived = lax.all_to_all(picked.reshape(-1, 8, width), E, 0, 0, tiled=True).reshape(rows, width)
    arrived, early = lax.optimization_barrier((arrived, ready(blocks[0], blocks[far])))
    other = swap_cores(arrived)
    parts = partial_sums(arrived, other, blocks, early)
    sums = lax.all_to_all(parts, "y", 0, 0, tiled=True)
    hidden = lax.all_to_all(hidden_copies(sums), "y", 0, 0, tiled=True)
    give = swap_cores(out_sums(hidden, blocks, width, False))
    keep = out_sums(hidden, blocks, width, True)
    result = (keep + give.astype(F32)).astype(BF)
    returned = lax.all_to_all(result.reshape(-1, 8, width), E, 0, 0, tiled=True)
    return finish(
        token_weights(names, gates, tokens.shape[0]),
        returned.reshape(rows, width),
        counts.reshape(-1, 1),
    )


def solution(mesh):
    fine = Mesh(np.asarray(mesh.devices).reshape(4, 16, NY, 2), ("x", "z", "y", "core"))
    return jax.shard_map(
        local,
        mesh=fine,
        in_specs=(
            P(E, None),
            P(None, E, None),
            P(None, E, None),
            P(E),
            P(E, None, S),
            P(E, None, S),
            P(E, S, None),
        ),
        out_specs=P(E, S),
        check_vma=False,
    )
```

```python
import functools

import jax
import jax.numpy as jnp
import numpy as np
from jax import lax
from jax.experimental import pallas as pl
from jax.experimental.pallas import tpu as pltpu
from jax.sharding import Mesh, PartitionSpec as P

E = ("x", "z")
S = ("y", "core")
NY = 4
HS = 128
BF = jnp.bfloat16
F32 = jnp.float32
HINT = 60 * 10**9
VMEM_LIMIT = 32 * 1024 * 1024
WHOLE = 60 * 1024 * 1024

SMEM = pl.BlockSpec(memory_space=pltpu.SMEM)
VMEM = pl.BlockSpec(memory_space=pltpu.VMEM)
ANY = pl.BlockSpec(memory_space=pl.ANY)


def dot(a, b):
    return jnp.dot(a, b, preferred_element_type=F32)


def call(kernel, out_shape, in_specs, out_specs, flops=0, bytes_accessed=1 << 20, vmem=VMEM_LIMIT, **more):
    return pl.pallas_call(
        kernel,
        out_shape=out_shape,
        in_specs=in_specs,
        out_specs=out_specs,
        compiler_params=pltpu.CompilerParams(vmem_limit_bytes=vmem),
        cost_estimate=pl.CostEstimate(flops=flops, bytes_accessed=bytes_accessed, transcendentals=0),
        **more,
    )


def swap_cores(a):
    return lax.ppermute(a, "core", [(0, 1), (1, 0)])


def block_copies(to, gate, up, down, out, sems):
    group = out.shape[1]
    first = pl.multiple_of(to * group, group)
    copies = [
        pltpu.make_async_copy(gate.at[pl.ds(first, group)], out.at[0], sems.at[0]),
        pltpu.make_async_copy(up.at[pl.ds(first, group)], out.at[1], sems.at[1]),
    ]
    for j in range(group // HS):
        column = pl.multiple_of(first + j * HS, HS)
        copies.append(
            pltpu.make_async_copy(
                down.at[:, pl.ds(column, HS)], out.at[2, pl.ds(j * HS, HS)], sems.at[2 + j]
            )
        )
    return copies


def spread(values, rows):
    slots, experts = values.shape
    lane = lax.broadcasted_iota(jnp.int32, (experts, rows), 1)
    expert = lax.broadcasted_iota(jnp.int32, (experts, rows), 0)
    wide = dot(values.astype(BF), (lane // slots == expert).astype(BF))
    lane = lax.broadcasted_iota(jnp.int32, (slots, rows), 1)
    slot = lax.broadcasted_iota(jnp.int32, (slots, rows), 0)
    return jnp.sum(jnp.where(lane % slots == slot, wide, 0.0), axis=0, keepdims=True)


def position():
    return lax.axis_index("y"), lax.axis_index("core")


def start_kernel(far, slots_ref, tokens, gate, up, down, picked, block, slots, own, rows_out, held, sems, own_sems, out_sems):
    y, c = position()
    width = own.shape[1]
    local_tokens = tokens.shape[0]
    first = pl.multiple_of((y * 2 + c) * width, width)
    fetch_slots = pltpu.make_async_copy(slots_ref, slots, own_sems.at[0])
    fetch = pltpu.make_async_copy(tokens.at[:, pl.ds(first, width)], own, own_sems.at[1])
    fetch_slots.start()
    fetch.start()
    copies = block_copies(lax.rem(y + far, NY), gate, up, down, held, sems)
    for copy in copies:
        copy.start()
    rows = picked.shape[0]
    token = lax.broadcasted_iota(jnp.int32, (local_tokens, rows), 0).astype(F32)
    fetch_slots.wait()
    names = spread(slots[...].astype(F32), rows)
    hit = (names == token).astype(BF)
    fetch.wait()
    step = rows // 2
    sends = []
    for n in range(2):
        part = pl.ds(n * step, step)
        rows_out[part] = lax.dot_general(
            hit[:, n * step : (n + 1) * step], own[...], (((0,), (0,)), ((), ())), preferred_element_type=F32
        ).astype(BF)
        sends.append(pltpu.make_async_copy(rows_out.at[part], picked.at[part], out_sems.at[n]))
        sends[-1].start()
    for copy in copies:
        copy.wait()
    sends.append(pltpu.make_async_copy(held, block, out_sems.at[2]))
    sends[-1].start()
    for send in sends:
        send.wait()


def start(far, slots, tokens, gate, up, down):
    group = gate.shape[0] // NY
    width = tokens.shape[1] // (2 * NY)
    rows = slots.shape[0] * slots.shape[1]
    return call(
        functools.partial(start_kernel, far),
        (jax.ShapeDtypeStruct((rows, width), BF), jax.ShapeDtypeStruct((3, group, HS), BF)),
        [ANY] * 5,
        (ANY, ANY),
        bytes_accessed=5 << 20,
        vmem=WHOLE,
        scratch_shapes=[
            pltpu.VMEM(slots.shape, jnp.int32),
            pltpu.VMEM((tokens.shape[0], width), BF),
            pltpu.VMEM((rows, width), BF),
            pltpu.VMEM((3, group, HS), BF),
            pltpu.SemaphoreType.DMA((2 + group // HS,)),
            pltpu.SemaphoreType.DMA((2,)),
            pltpu.SemaphoreType.DMA((3,)),
        ],
    )(slots, tokens, gate, up, down)


def pack_kernel(d, gate, up, down, out, sems):
    copies = block_copies(lax.rem(position()[0] + d, NY), gate, up, down, out, sems)
    for copy in copies:
        copy.start()
    for copy in copies:
        copy.wait()


def pack(d, gate, up, down):
    group = gate.shape[0] // NY
    return call(
        functools.partial(pack_kernel, d),
        jax.ShapeDtypeStruct((3, group, HS), BF),
        [ANY, ANY, ANY],
        VMEM,
        vmem=WHOLE,
        scratch_shapes=[pltpu.SemaphoreType.DMA((2 + group // HS,))],
    )(gate, up, down)


def ready_kernel(first, second, out, sem):
    copy = pltpu.make_async_copy(first.at[0, pl.ds(0, out.shape[0])], out, sem)
    copy.start()
    copy.wait()


def ready(first, second):
    return call(
        ready_kernel,
        jax.ShapeDtypeStruct((16, HS), BF),
        [ANY, ANY],
        VMEM,
        flops=HINT,
        scratch_shapes=[pltpu.SemaphoreType.DMA],
    )(first, second)


def half_kernel(rows, w0, w1, w2, w3, early, out):
    y, c = position()
    width = rows.shape[1]
    step = 256
    part = pl.ds(pl.multiple_of(c * width, width), width)
    for d, w in enumerate((w0, w1, w2, w3)):
        owner = lax.rem(y + NY - d, NY)
        a = jnp.concatenate([w[0, part], w[1, part]], axis=1)
        for r in range(0, rows.shape[0], step):
            at = pl.ds(r, step)
            out[owner, at] = dot(rows[at], a)


def whole_kernel(rows, w0, w1, w2, w3, half, out):
    y, c = position()
    width = rows.shape[1]
    step = 256
    part = pl.ds(pl.multiple_of((1 - c) * width, width), width)
    for d, w in enumerate((w0, w1, w2, w3)):
        owner = lax.rem(y + NY - d, NY)
        a = jnp.concatenate([w[0, part], w[1, part]], axis=1)
        for r in range(0, rows.shape[0], step):
            at = pl.ds(r, step)
            out[owner, at] = (half[owner, at] + dot(rows[at], a)).astype(BF)


def partial_sums(own, other, blocks, early):
    rows, width = own.shape
    shape = (NY, rows, 2 * HS)
    flops = 2 * rows * width * NY * 2 * HS
    half = call(
        half_kernel, jax.ShapeDtypeStruct(shape, F32), [VMEM] * 5 + [ANY], VMEM, flops=flops
    )(own, *blocks, early)
    return call(whole_kernel, jax.ShapeDtypeStruct(shape, BF), [VMEM] * 6, VMEM, flops=flops)(
        other, *blocks, half
    )


def hidden_kernel(sums, out):
    total = sums[0].astype(F32)
    for k in range(1, NY):
        total = total + sums[k].astype(F32)
    gate, up = total[:, :HS], total[:, HS:]
    hidden = (gate / (1.0 + jnp.exp(-gate)) * up).astype(BF)
    for k in range(NY):
        out[k] = hidden


def hidden_copies(sums):
    return call(
        hidden_kernel, jax.ShapeDtypeStruct((NY, sums.shape[1], HS), BF), [VMEM], VMEM
    )(sums)


def out_kernel(mine, hidden, w0, w1, w2, w3, out):
    y, c = position()
    rows = hidden.shape[1]
    width = out.shape[1]
    first = (c if mine else 1 - c) * width
    owners = [lax.rem(y + NY - d, NY) for d in range(NY)]
    a = jnp.concatenate([hidden[k] for k in owners], axis=1)
    for j in range(0, width, 2 * HS):
        one = pl.multiple_of(first + j, HS)
        two = pl.multiple_of(first + j + HS, HS)
        b = jnp.concatenate(
            [
                jnp.concatenate([w[2, pl.ds(one, HS)], w[2, pl.ds(two, HS)]], axis=1)
                for w in (w0, w1, w2, w3)
            ],
            axis=0,
        )
        out[:, pl.ds(j, 2 * HS)] = dot(a, b).astype(out.dtype)


def out_sums(hidden, blocks, width, mine):
    rows = hidden.shape[1]
    return call(
        functools.partial(out_kernel, mine),
        jax.ShapeDtypeStruct((rows, width), F32 if mine else BF),
        [VMEM] * 5,
        VMEM,
        flops=2 * rows * width * NY * HS,
    )(hidden, *blocks)


def result_kernel(keep, given, out, sums, sems):
    rows = keep.shape[0]
    step = rows // 4
    sends = []
    for n in range(4):
        part = pl.ds(n * step, step)
        sums[part] = (keep[part] + given[part].astype(F32)).astype(BF)
        sends.append(pltpu.make_async_copy(sums.at[part], out.at[part], sems.at[n]))
        sends[-1].start()
    for send in sends:
        send.wait()


def result_rows(keep, given):
    return call(
        result_kernel,
        jax.ShapeDtypeStruct(given.shape, BF),
        [VMEM, VMEM],
        ANY,
        scratch_shapes=[pltpu.VMEM(given.shape, BF), pltpu.SemaphoreType.DMA((4,))],
    )(keep, given)


def weight_kernel(slots, gates, counts, out):
    tokens, rows = out.shape[1:]
    names = spread(slots[...].astype(F32), rows)
    hit = names == lax.broadcasted_iota(jnp.int32, (tokens, rows), 0).astype(F32)
    left = gates[...]
    gate = jnp.zeros((1, rows), F32)
    for p in range(3):
        piece = left.astype(BF).astype(F32)
        left = left - piece
        gate = gate + spread(piece, rows)
    left = jnp.where(hit, gate, 0.0) / jnp.maximum(counts[...].astype(F32), 1.0)
    for p in range(out.shape[0]):
        piece = left.astype(BF)
        left = left - piece.astype(F32)
        out[p] = piece


def token_weights(slots, gates, counts):
    rows = slots.shape[0] * slots.shape[1]
    return call(
        weight_kernel, jax.ShapeDtypeStruct((3, counts.shape[0], rows), BF), [VMEM] * 3, VMEM
    )(slots, gates, counts)


def finish_kernel(weights, returned, out):
    rows = returned[...]
    total = dot(weights[2], rows) + dot(weights[1], rows)
    out[...] = (total + dot(weights[0], rows)).astype(BF)


def finish(weights, returned):
    return call(
        finish_kernel,
        jax.ShapeDtypeStruct((weights.shape[1], returned.shape[1]), BF),
        [VMEM] * 2,
        VMEM,
    )(weights, returned)


def local(tokens, slot_lists, slot_gates, counts, gate_weight, up_weight, down_weight):
    width = tokens.shape[1] // (2 * NY)
    experts, _, slots = slot_lists.shape
    rows = experts * slots
    weights = gate_weight[0], up_weight[0], down_weight[0]
    names = slot_lists.transpose(2, 1, 0).reshape(slots, experts)
    gates = slot_gates.transpose(2, 1, 0).reshape(slots, experts)

    far = 2
    picked, first = start(far, names, tokens, *weights)
    blocks = []
    for d in range(NY):
        block = first if d == far else pack(d, *weights)
        blocks.append(lax.ppermute(block, "y", [(j, (j + d) % NY) for j in range(NY)]) if d else block)
    arrived = lax.all_to_all(picked.reshape(-1, 8, width), E, 0, 0, tiled=True).reshape(rows, width)
    arrived, early = lax.optimization_barrier((arrived, ready(blocks[0], blocks[far])))
    other = swap_cores(arrived)
    parts = partial_sums(arrived, other, blocks, early)
    sums = lax.all_to_all(parts, "y", 0, 0, tiled=True)
    hidden = lax.all_to_all(hidden_copies(sums), "y", 0, 0, tiled=True)
    give = swap_cores(out_sums(hidden, blocks, width, False))
    keep = out_sums(hidden, blocks, width, True)
    result = result_rows(keep, give)
    returned = lax.all_to_all(result.reshape(-1, 8, width), E, 0, 0, tiled=True)
    return finish(token_weights(names, gates, counts.reshape(-1, 1)), returned.reshape(rows, width))


def solution(mesh):
    fine = Mesh(np.asarray(mesh.devices).reshape(4, 16, NY, 2), ("x", "z", "y", "core"))
    return jax.shard_map(
        local,
        mesh=fine,
        in_specs=(
            P(E, None),
            P(None, E, None),
            P(None, E, None),
            P(E),
            P(E, None, S),
            P(E, None, S),
            P(E, S, None),
        ),
        out_specs=P(E, S),
        check_vma=False,
    )
```

```python
import functools

import jax
import jax.numpy as jnp
import numpy as np
from jax import lax
from jax.experimental import pallas as pl
from jax.experimental.pallas import tpu as pltpu
from jax.sharding import Mesh, PartitionSpec as P

E = "expert"
NX, NZ = 4, 16
X0, Z0, Y0 = 0, 11, 2
S = ("y", "core")
NY = 4
HS = 128
BF = jnp.bfloat16
F32 = jnp.float32
HINT = 60 * 10**9
VMEM_LIMIT = 32 * 1024 * 1024
WHOLE = 60 * 1024 * 1024

SMEM = pl.BlockSpec(memory_space=pltpu.SMEM)
VMEM = pl.BlockSpec(memory_space=pltpu.VMEM)
ANY = pl.BlockSpec(memory_space=pl.ANY)


def dot(a, b):
    return jnp.dot(a, b, preferred_element_type=F32)


def call(kernel, out_shape, in_specs, out_specs, flops=0, bytes_accessed=1 << 20, vmem=VMEM_LIMIT, **more):
    return pl.pallas_call(
        kernel,
        out_shape=out_shape,
        in_specs=in_specs,
        out_specs=out_specs,
        compiler_params=pltpu.CompilerParams(vmem_limit_bytes=vmem),
        cost_estimate=pl.CostEstimate(flops=flops, bytes_accessed=bytes_accessed, transcendentals=0),
        **more,
    )


def swap_cores(a):
    return lax.ppermute(a, "core", [(0, 1), (1, 0)])


def block_copies(to, gate, up, down, out, sems):
    group = out.shape[1]
    first = pl.multiple_of(to * group, group)
    copies = [
        pltpu.make_async_copy(gate.at[pl.ds(first, group)], out.at[0], sems.at[0]),
        pltpu.make_async_copy(up.at[pl.ds(first, group)], out.at[1], sems.at[1]),
    ]
    for j in range(group // HS):
        column = pl.multiple_of(first + j * HS, HS)
        copies.append(
            pltpu.make_async_copy(
                down.at[:, pl.ds(column, HS)], out.at[2, pl.ds(j * HS, HS)], sems.at[2 + j]
            )
        )
    return copies


def expert_at(place):
    return (place // NZ + X0) % NX * NZ + (place % NZ + Z0) % NZ


def exchange(rows):
    order = [expert_at(place) for place in range(rows.shape[0])]
    return lax.all_to_all(rows, E, 0, 0, axis_index_groups=[order], tiled=True)


def exchange_y(blocks):
    order = [(place + Y0) % NY for place in range(NY)]
    return lax.all_to_all(blocks, "y", 0, 0, axis_index_groups=[order], tiled=True)


def place_y(y, d):
    return lax.rem(y + 2 * NY - d - Y0, NY)


def spread(values, rows):
    slots, experts = values.shape
    lane = lax.broadcasted_iota(jnp.int32, (experts, rows), 1)
    expert = lax.broadcasted_iota(jnp.int32, (experts, rows), 0)
    wide = dot(values.astype(BF), (expert_at(lane // slots) == expert).astype(BF))
    lane = lax.broadcasted_iota(jnp.int32, (slots, rows), 1)
    slot = lax.broadcasted_iota(jnp.int32, (slots, rows), 0)
    return jnp.sum(jnp.where(lane % slots == slot, wide, 0.0), axis=0, keepdims=True)


def position():
    return lax.axis_index("y"), lax.axis_index("core")


def start_kernel(far, slots_ref, tokens, gate, up, down, picked, block, slots, own, rows_out, held, sems, own_sems, out_sems):
    y, c = position()
    width = own.shape[1]
    local_tokens = tokens.shape[0]
    first = pl.multiple_of((y * 2 + c) * width, width)
    fetch_slots = pltpu.make_async_copy(slots_ref, slots, own_sems.at[0])
    fetch = pltpu.make_async_copy(tokens.at[:, pl.ds(first, width)], own, own_sems.at[1])
    fetch_slots.start()
    fetch.start()
    copies = block_copies(lax.rem(y + far, NY), gate, up, down, held, sems)
    for copy in copies:
        copy.start()
    rows = picked.shape[0]
    token = lax.broadcasted_iota(jnp.int32, (local_tokens, rows), 0).astype(F32)
    fetch_slots.wait()
    names = spread(slots[...].astype(F32), rows)
    hit = (names == token).astype(BF)
    fetch.wait()
    step = rows // 4
    sends = []
    for n in range(4):
        part = pl.ds(n * step, step)
        rows_out[part] = lax.dot_general(
            hit[:, n * step : (n + 1) * step], own[...], (((0,), (0,)), ((), ())), preferred_element_type=F32
        ).astype(BF)
        sends.append(pltpu.make_async_copy(rows_out.at[part], picked.at[part], out_sems.at[n]))
        sends[-1].start()
    for copy in copies:
        copy.wait()
    sends.append(pltpu.make_async_copy(held, block, out_sems.at[4]))
    sends[-1].start()
    for send in sends:
        send.wait()


def start(far, slots, tokens, gate, up, down):
    group = gate.shape[0] // NY
    width = tokens.shape[1] // (2 * NY)
    rows = slots.shape[0] * slots.shape[1]
    return call(
        functools.partial(start_kernel, far),
        (jax.ShapeDtypeStruct((rows, width), BF), jax.ShapeDtypeStruct((3, group, HS), BF)),
        [ANY] * 5,
        (ANY, ANY),
        bytes_accessed=5 << 20,
        vmem=WHOLE,
        scratch_shapes=[
            pltpu.VMEM(slots.shape, jnp.int32),
            pltpu.VMEM((tokens.shape[0], width), BF),
            pltpu.VMEM((rows, width), BF),
            pltpu.VMEM((3, group, HS), BF),
            pltpu.SemaphoreType.DMA((2 + group // HS,)),
            pltpu.SemaphoreType.DMA((2,)),
            pltpu.SemaphoreType.DMA((5,)),
        ],
    )(slots, tokens, gate, up, down)


def pack_kernel(d, gate, up, down, out, sems):
    copies = block_copies(lax.rem(position()[0] + d, NY), gate, up, down, out, sems)
    for copy in copies:
        copy.start()
    for copy in copies:
        copy.wait()


def pack(d, gate, up, down):
    group = gate.shape[0] // NY
    return call(
        functools.partial(pack_kernel, d),
        jax.ShapeDtypeStruct((3, group, HS), BF),
        [ANY, ANY, ANY],
        VMEM,
        vmem=WHOLE,
        scratch_shapes=[pltpu.SemaphoreType.DMA((2 + group // HS,))],
    )(gate, up, down)


def ready_kernel(first, second, out, sem):
    copy = pltpu.make_async_copy(first.at[0, pl.ds(0, out.shape[0])], out, sem)
    copy.start()
    copy.wait()


def ready(first, second):
    return call(
        ready_kernel,
        jax.ShapeDtypeStruct((16, HS), BF),
        [ANY, ANY],
        VMEM,
        flops=HINT,
        scratch_shapes=[pltpu.SemaphoreType.DMA],
    )(first, second)


def half_kernel(rows, w0, w1, w2, w3, early, out):
    y, c = position()
    width = rows.shape[1]
    step = 256
    part = pl.ds(pl.multiple_of(c * width, width), width)
    for d, w in enumerate((w0, w1, w2, w3)):
        owner = place_y(y, d)
        a = jnp.concatenate([w[0, part], w[1, part]], axis=1)
        for r in range(0, rows.shape[0], step):
            at = pl.ds(r, step)
            out[owner, at] = dot(rows[at], a)


def whole_kernel(rows, w0, w1, w2, w3, half, out):
    y, c = position()
    width = rows.shape[1]
    step = 256
    part = pl.ds(pl.multiple_of((1 - c) * width, width), width)
    for d, w in enumerate((w0, w1, w2, w3)):
        owner = place_y(y, d)
        a = jnp.concatenate([w[0, part], w[1, part]], axis=1)
        for r in range(0, rows.shape[0], step):
            at = pl.ds(r, step)
            out[owner, at] = (half[owner, at] + dot(rows[at], a)).astype(BF)


def partial_sums(own, other, blocks, early):
    rows, width = own.shape
    shape = (NY, rows, 2 * HS)
    flops = 2 * rows * width * NY * 2 * HS
    half = call(
        half_kernel, jax.ShapeDtypeStruct(shape, F32), [VMEM] * 5 + [ANY], VMEM, flops=flops
    )(own, *blocks, early)
    return call(whole_kernel, jax.ShapeDtypeStruct(shape, BF), [VMEM] * 6, VMEM, flops=flops)(
        other, *blocks, half
    )


def hidden_kernel(sums, out):
    total = sums[0].astype(F32)
    for k in range(1, NY):
        total = total + sums[k].astype(F32)
    gate, up = total[:, :HS], total[:, HS:]
    hidden = (gate / (1.0 + jnp.exp(-gate)) * up).astype(BF)
    for k in range(NY):
        out[k] = hidden


def hidden_copies(sums):
    return call(
        hidden_kernel, jax.ShapeDtypeStruct((NY, sums.shape[1], HS), BF), [VMEM], VMEM
    )(sums)


def out_kernel(mine, hidden, w0, w1, w2, w3, out):
    y, c = position()
    rows = hidden.shape[1]
    width = out.shape[1]
    first = (c if mine else 1 - c) * width
    owners = [place_y(y, d) for d in range(NY)]
    a = jnp.concatenate([hidden[k] for k in owners], axis=1)
    for j in range(0, width, 2 * HS):
        one = pl.multiple_of(first + j, HS)
        two = pl.multiple_of(first + j + HS, HS)
        b = jnp.concatenate(
            [
                jnp.concatenate([w[2, pl.ds(one, HS)], w[2, pl.ds(two, HS)]], axis=1)
                for w in (w0, w1, w2, w3)
            ],
            axis=0,
        )
        out[:, pl.ds(j, 2 * HS)] = dot(a, b).astype(out.dtype)


def out_sums(hidden, blocks, width, mine):
    rows = hidden.shape[1]
    return call(
        functools.partial(out_kernel, mine),
        jax.ShapeDtypeStruct((rows, width), F32 if mine else BF),
        [VMEM] * 5,
        VMEM,
        flops=2 * rows * width * NY * HS,
    )(hidden, *blocks)


def result_kernel(keep, given, out, sums, sems):
    rows = keep.shape[0]
    step = rows // 4
    sends = []
    for n in range(4):
        part = pl.ds(n * step, step)
        sums[part] = (keep[part] + given[part].astype(F32)).astype(BF)
        sends.append(pltpu.make_async_copy(sums.at[part], out.at[part], sems.at[n]))
        sends[-1].start()
    for send in sends:
        send.wait()


def result_rows(keep, given):
    return call(
        result_kernel,
        jax.ShapeDtypeStruct(given.shape, BF),
        [VMEM, VMEM],
        ANY,
        scratch_shapes=[pltpu.VMEM(given.shape, BF), pltpu.SemaphoreType.DMA((4,))],
    )(keep, given)


def weight_kernel(slots, gates, counts, out):
    tokens, rows = out.shape[1:]
    names = spread(slots[...].astype(F32), rows)
    hit = names == lax.broadcasted_iota(jnp.int32, (tokens, rows), 0).astype(F32)
    left = gates[...]
    gate = jnp.zeros((1, rows), F32)
    for p in range(3):
        piece = left.astype(BF).astype(F32)
        left = left - piece
        gate = gate + spread(piece, rows)
    left = jnp.where(hit, gate, 0.0) / jnp.maximum(counts[...].astype(F32), 1.0)
    high = left.astype(BF)
    out[0] = high
    out[1] = (left - high.astype(F32)).astype(BF)


def token_weights(slots, gates, counts):
    rows = slots.shape[0] * slots.shape[1]
    return call(
        weight_kernel, jax.ShapeDtypeStruct((2, counts.shape[0], rows), BF), [VMEM] * 3, VMEM
    )(slots, gates, counts)


def finish_kernel(weights, returned, out, held, sems):
    tokens, width = held.shape
    step = width // 2
    high, low = weights[0], weights[1]
    sends = []
    for n in range(2):
        part = pl.ds(n * step, step)
        rows = returned[:, part]
        held[:, part] = (dot(low, rows) + dot(high, rows)).astype(BF)
        sends.append(pltpu.make_async_copy(held.at[:, part], out.at[:, part], sems.at[n]))
        sends[-1].start()
    for send in sends:
        send.wait()


def finish(weights, returned):
    shape = (weights.shape[1], returned.shape[1])
    return call(
        finish_kernel,
        jax.ShapeDtypeStruct(shape, BF),
        [VMEM] * 2,
        ANY,
        scratch_shapes=[pltpu.VMEM(shape, BF), pltpu.SemaphoreType.DMA((2,))],
    )(weights, returned)


def local(tokens, slot_lists, slot_gates, counts, gate_weight, up_weight, down_weight):
    width = tokens.shape[1] // (2 * NY)
    experts, _, slots = slot_lists.shape
    rows = experts * slots
    weights = gate_weight[0], up_weight[0], down_weight[0]
    names = slot_lists.transpose(2, 1, 0).reshape(slots, experts)
    gates = slot_gates.transpose(2, 1, 0).reshape(slots, experts)

    far = 2
    picked, first = start(far, names, tokens, *weights)
    blocks = []
    for d in range(NY):
        block = first if d == far else pack(d, *weights)
        blocks.append(lax.ppermute(block, "y", [(j, (j + d) % NY) for j in range(NY)]) if d else block)
    arrived = exchange(picked.reshape(-1, 8, width)).reshape(rows, width)
    arrived, early = lax.optimization_barrier((arrived, ready(blocks[0], blocks[far])))
    other = swap_cores(arrived)
    parts = partial_sums(arrived, other, blocks, early)
    sums = exchange_y(parts)
    hidden = exchange_y(hidden_copies(sums))
    give = swap_cores(out_sums(hidden, blocks, width, False))
    keep = out_sums(hidden, blocks, width, True)
    result = result_rows(keep, give)
    returned = exchange(result.reshape(-1, 8, width))
    return finish(token_weights(names, gates, counts.reshape(-1, 1)), returned.reshape(rows, width))


def solution(mesh):
    fine = Mesh(np.asarray(mesh.devices).reshape(NX * NZ, NY, 2), (E, "y", "core"))
    return jax.shard_map(
        local,
        mesh=fine,
        in_specs=(
            P(E, None),
            P(None, E, None),
            P(None, E, None),
            P(E),
            P(E, None, S),
            P(E, None, S),
            P(E, S, None),
        ),
        out_specs=P(E, S),
        check_vma=False,
    )
```

```python
import functools

import jax
import jax.numpy as jnp
import numpy as np
from jax import lax
from jax.experimental import pallas as pl
from jax.experimental.pallas import tpu as pltpu
from jax.sharding import Mesh, PartitionSpec as P

E = "expert"
NX, NZ = 4, 16
X0, Z0, Y_SUMS, Y_HIDDEN = 0, 11, 3, 2
S = ("y", "core")
NY = 4
HS = 128
BF = jnp.bfloat16
F32 = jnp.float32
HINT = 60 * 10**9
VMEM_LIMIT = 32 * 1024 * 1024
WHOLE = 60 * 1024 * 1024

SMEM = pl.BlockSpec(memory_space=pltpu.SMEM)
VMEM = pl.BlockSpec(memory_space=pltpu.VMEM)
ANY = pl.BlockSpec(memory_space=pl.ANY)


def dot(a, b):
    return jnp.dot(a, b, preferred_element_type=F32)


def call(kernel, out_shape, in_specs, out_specs, flops=0, bytes_accessed=1 << 20, vmem=VMEM_LIMIT, **more):
    return pl.pallas_call(
        kernel,
        out_shape=out_shape,
        in_specs=in_specs,
        out_specs=out_specs,
        compiler_params=pltpu.CompilerParams(vmem_limit_bytes=vmem),
        cost_estimate=pl.CostEstimate(flops=flops, bytes_accessed=bytes_accessed, transcendentals=0),
        **more,
    )


def swap_cores(a):
    return lax.ppermute(a, "core", [(0, 1), (1, 0)])


def block_copies(to, gate, up, down, out, sems):
    group = out.shape[1]
    first = pl.multiple_of(to * group, group)
    copies = [
        pltpu.make_async_copy(gate.at[pl.ds(first, group)], out.at[0], sems.at[0]),
        pltpu.make_async_copy(up.at[pl.ds(first, group)], out.at[1], sems.at[1]),
    ]
    for j in range(group // HS):
        column = pl.multiple_of(first + j * HS, HS)
        copies.append(
            pltpu.make_async_copy(
                down.at[:, pl.ds(column, HS)], out.at[2, pl.ds(j * HS, HS)], sems.at[2 + j]
            )
        )
    return copies


def expert_at(place):
    return (place // NZ + X0) % NX * NZ + (place % NZ + Z0) % NZ


def exchange(rows):
    order = [expert_at(place) for place in range(rows.shape[0])]
    return lax.all_to_all(rows, E, 0, 0, axis_index_groups=[order], tiled=True)


def exchange_y(blocks, y0):
    order = [(place + y0) % NY for place in range(NY)]
    return lax.all_to_all(blocks, "y", 0, 0, axis_index_groups=[order], tiled=True)


def place_y(y, d, y0):
    return lax.rem(y + 2 * NY - d - y0, NY)


def spread(values, rows):
    slots, experts = values.shape
    lane = lax.broadcasted_iota(jnp.int32, (experts, rows), 1)
    expert = lax.broadcasted_iota(jnp.int32, (experts, rows), 0)
    wide = dot(values.astype(BF), (expert_at(lane // slots) == expert).astype(BF))
    lane = lax.broadcasted_iota(jnp.int32, (slots, rows), 1)
    slot = lax.broadcasted_iota(jnp.int32, (slots, rows), 0)
    return jnp.sum(jnp.where(lane % slots == slot, wide, 0.0), axis=0, keepdims=True)


def position():
    return lax.axis_index("y"), lax.axis_index("core")


def start_kernel(far, slots_ref, tokens, gate, up, down, picked, block, slots, own, rows_out, held, sems, own_sems, out_sems):
    y, c = position()
    width = own.shape[1]
    local_tokens = tokens.shape[0]
    first = pl.multiple_of((y * 2 + c) * width, width)
    fetch_slots = pltpu.make_async_copy(slots_ref, slots, own_sems.at[0])
    fetch = pltpu.make_async_copy(tokens.at[:, pl.ds(first, width)], own, own_sems.at[1])
    fetch_slots.start()
    fetch.start()
    copies = block_copies(lax.rem(y + far, NY), gate, up, down, held, sems)
    for copy in copies:
        copy.start()
    rows = picked.shape[0]
    token = lax.broadcasted_iota(jnp.int32, (local_tokens, rows), 0).astype(F32)
    fetch_slots.wait()
    names = spread(slots[...].astype(F32), rows)
    hit = (names == token).astype(BF)
    for copy in copies:
        copy.wait()
    sends = [pltpu.make_async_copy(held, block, out_sems.at[4])]
    sends[0].start()
    fetch.wait()
    step = rows // 4
    for n in range(4):
        part = pl.ds(n * step, step)
        rows_out[part] = lax.dot_general(
            hit[:, n * step : (n + 1) * step], own[...], (((0,), (0,)), ((), ())), preferred_element_type=F32
        ).astype(BF)
        sends.append(pltpu.make_async_copy(rows_out.at[part], picked.at[part], out_sems.at[n]))
        sends[-1].start()
    for send in sends:
        send.wait()


def start(far, slots, tokens, gate, up, down):
    group = gate.shape[0] // NY
    width = tokens.shape[1] // (2 * NY)
    rows = slots.shape[0] * slots.shape[1]
    return call(
        functools.partial(start_kernel, far),
        (jax.ShapeDtypeStruct((rows, width), BF), jax.ShapeDtypeStruct((3, group, HS), BF)),
        [ANY] * 5,
        (ANY, ANY),
        bytes_accessed=5 << 20,
        vmem=WHOLE,
        scratch_shapes=[
            pltpu.VMEM(slots.shape, jnp.int32),
            pltpu.VMEM((tokens.shape[0], width), BF),
            pltpu.VMEM((rows, width), BF),
            pltpu.VMEM((3, group, HS), BF),
            pltpu.SemaphoreType.DMA((2 + group // HS,)),
            pltpu.SemaphoreType.DMA((2,)),
            pltpu.SemaphoreType.DMA((5,)),
        ],
    )(slots, tokens, gate, up, down)


def pack_kernel(d, gate, up, down, out, sems):
    copies = block_copies(lax.rem(position()[0] + d, NY), gate, up, down, out, sems)
    for copy in copies:
        copy.start()
    for copy in copies:
        copy.wait()


def pack(d, gate, up, down):
    group = gate.shape[0] // NY
    return call(
        functools.partial(pack_kernel, d),
        jax.ShapeDtypeStruct((3, group, HS), BF),
        [ANY, ANY, ANY],
        VMEM,
        vmem=WHOLE,
        scratch_shapes=[pltpu.SemaphoreType.DMA((2 + group // HS,))],
    )(gate, up, down)


def ready_kernel(first, second, out, sem):
    copy = pltpu.make_async_copy(first.at[0, pl.ds(0, out.shape[0])], out, sem)
    copy.start()
    copy.wait()


def ready(first, second):
    return call(
        ready_kernel,
        jax.ShapeDtypeStruct((16, HS), BF),
        [ANY, ANY],
        VMEM,
        flops=HINT,
        scratch_shapes=[pltpu.SemaphoreType.DMA],
    )(first, second)


def half_kernel(rows, w0, w1, w2, w3, early, out):
    y, c = position()
    width = rows.shape[1]
    step = 256
    part = pl.ds(pl.multiple_of(c * width, width), width)
    for d, w in enumerate((w0, w1, w2, w3)):
        owner = place_y(y, d, Y_SUMS)
        a = jnp.concatenate([w[0, part], w[1, part]], axis=1)
        for r in range(0, rows.shape[0], step):
            at = pl.ds(r, step)
            out[owner, at] = dot(rows[at], a)


def whole_kernel(rows, w0, w1, w2, w3, half, out):
    y, c = position()
    width = rows.shape[1]
    step = 256
    part = pl.ds(pl.multiple_of((1 - c) * width, width), width)
    for d, w in enumerate((w0, w1, w2, w3)):
        owner = place_y(y, d, Y_SUMS)
        a = jnp.concatenate([w[0, part], w[1, part]], axis=1)
        for r in range(0, rows.shape[0], step):
            at = pl.ds(r, step)
            out[owner, at] = (half[owner, at] + dot(rows[at], a)).astype(BF)


def partial_sums(own, other, blocks, early):
    rows, width = own.shape
    shape = (NY, rows, 2 * HS)
    flops = 2 * rows * width * NY * 2 * HS
    half = call(
        half_kernel, jax.ShapeDtypeStruct(shape, F32), [VMEM] * 5 + [ANY], VMEM, flops=flops
    )(own, *blocks, early)
    return call(whole_kernel, jax.ShapeDtypeStruct(shape, BF), [VMEM] * 6, VMEM, flops=flops)(
        other, *blocks, half
    )


def hidden_kernel(sums, out):
    total = sums[0].astype(F32)
    for k in range(1, NY):
        total = total + sums[k].astype(F32)
    gate, up = total[:, :HS], total[:, HS:]
    hidden = (gate / (1.0 + jnp.exp(-gate)) * up).astype(BF)
    for k in range(NY):
        out[k] = hidden


def hidden_copies(sums):
    return call(
        hidden_kernel, jax.ShapeDtypeStruct((NY, sums.shape[1], HS), BF), [VMEM], VMEM
    )(sums)


def out_kernel(mine, hidden, w0, w1, w2, w3, out):
    y, c = position()
    rows = hidden.shape[1]
    width = out.shape[1]
    first = (c if mine else 1 - c) * width
    owners = [place_y(y, d, Y_HIDDEN) for d in range(NY)]
    a = jnp.concatenate([hidden[k] for k in owners], axis=1)
    for j in range(0, width, 2 * HS):
        one = pl.multiple_of(first + j, HS)
        two = pl.multiple_of(first + j + HS, HS)
        b = jnp.concatenate(
            [
                jnp.concatenate([w[2, pl.ds(one, HS)], w[2, pl.ds(two, HS)]], axis=1)
                for w in (w0, w1, w2, w3)
            ],
            axis=0,
        )
        out[:, pl.ds(j, 2 * HS)] = dot(a, b).astype(out.dtype)


def out_sums(hidden, blocks, width, mine):
    rows = hidden.shape[1]
    return call(
        functools.partial(out_kernel, mine),
        jax.ShapeDtypeStruct((rows, width), F32 if mine else BF),
        [VMEM] * 5,
        VMEM,
        flops=2 * rows * width * NY * HS,
    )(hidden, *blocks)


def result_kernel(keep, given, out, sums, sems):
    rows = keep.shape[0]
    step = rows // 4
    sends = []
    for n in range(4):
        part = pl.ds(n * step, step)
        sums[part] = (keep[part] + given[part].astype(F32)).astype(BF)
        sends.append(pltpu.make_async_copy(sums.at[part], out.at[part], sems.at[n]))
        sends[-1].start()
    for send in sends:
        send.wait()


def result_rows(keep, given):
    return call(
        result_kernel,
        jax.ShapeDtypeStruct(given.shape, BF),
        [VMEM, VMEM],
        ANY,
        scratch_shapes=[pltpu.VMEM(given.shape, BF), pltpu.SemaphoreType.DMA((4,))],
    )(keep, given)


def weight_kernel(slots, gates, counts, out):
    tokens, rows = out.shape[1:]
    names = spread(slots[...].astype(F32), rows)
    hit = names == lax.broadcasted_iota(jnp.int32, (tokens, rows), 0).astype(F32)
    left = gates[...]
    gate = jnp.zeros((1, rows), F32)
    for p in range(3):
        piece = left.astype(BF).astype(F32)
        left = left - piece
        gate = gate + spread(piece, rows)
    left = jnp.where(hit, gate, 0.0) / jnp.maximum(counts[...].astype(F32), 1.0)
    high = left.astype(BF)
    out[0] = high
    out[1] = (left - high.astype(F32)).astype(BF)


def token_weights(slots, gates, counts):
    rows = slots.shape[0] * slots.shape[1]
    return call(
        weight_kernel, jax.ShapeDtypeStruct((2, counts.shape[0], rows), BF), [VMEM] * 3, VMEM
    )(slots, gates, counts)


def finish_kernel(weights, returned, out, held, sems):
    tokens, width = held.shape
    step = width // 2
    high, low = weights[0], weights[1]
    sends = []
    for n in range(2):
        part = pl.ds(n * step, step)
        rows = returned[:, part]
        held[:, part] = (dot(low, rows) + dot(high, rows)).astype(BF)
        sends.append(pltpu.make_async_copy(held.at[:, part], out.at[:, part], sems.at[n]))
        sends[-1].start()
    for send in sends:
        send.wait()


def finish(weights, returned):
    shape = (weights.shape[1], returned.shape[1])
    return call(
        finish_kernel,
        jax.ShapeDtypeStruct(shape, BF),
        [VMEM] * 2,
        ANY,
        scratch_shapes=[pltpu.VMEM(shape, BF), pltpu.SemaphoreType.DMA((2,))],
    )(weights, returned)


def local(tokens, slot_lists, slot_gates, counts, gate_weight, up_weight, down_weight):
    width = tokens.shape[1] // (2 * NY)
    experts, _, slots = slot_lists.shape
    rows = experts * slots
    weights = gate_weight[0], up_weight[0], down_weight[0]
    names = slot_lists.transpose(2, 1, 0).reshape(slots, experts)
    gates = slot_gates.transpose(2, 1, 0).reshape(slots, experts)

    far = 2
    picked, first = start(far, names, tokens, *weights)
    blocks = []
    for d in range(NY):
        block = first if d == far else pack(d, *weights)
        blocks.append(lax.ppermute(block, "y", [(j, (j + d) % NY) for j in range(NY)]) if d else block)
    arrived = exchange(picked.reshape(-1, 8, width)).reshape(rows, width)
    arrived, early = lax.optimization_barrier((arrived, ready(blocks[0], blocks[far])))
    other = swap_cores(arrived)
    parts = partial_sums(arrived, other, blocks, early)
    sums = exchange_y(parts, Y_SUMS)
    hidden = exchange_y(hidden_copies(sums), Y_HIDDEN)
    give = swap_cores(out_sums(hidden, blocks, width, False))
    keep = out_sums(hidden, blocks, width, True)
    result = result_rows(keep, give)
    returned = exchange(result.reshape(-1, 8, width))
    return finish(token_weights(names, gates, counts.reshape(-1, 1)), returned.reshape(rows, width))


def solution(mesh):
    fine = Mesh(np.asarray(mesh.devices).reshape(NX * NZ, NY, 2), (E, "y", "core"))
    return jax.shard_map(
        local,
        mesh=fine,
        in_specs=(
            P(E, None),
            P(None, E, None),
            P(None, E, None),
            P(E),
            P(E, None, S),
            P(E, None, S),
            P(E, S, None),
        ),
        out_specs=P(E, S),
        check_vma=False,
    )
```

```python
import functools

import jax
import jax.numpy as jnp
import numpy as np
from jax import lax
from jax.experimental import pallas as pl
from jax.experimental.pallas import tpu as pltpu
from jax.sharding import Mesh, PartitionSpec as P

E = "expert"
NX, NZ = 4, 16
X0, Z0, Y_SUMS, Y_HIDDEN = 0, 11, 3, 2
S = ("y", "core")
NY = 4
HS = 128
BF = jnp.bfloat16
F32 = jnp.float32
HINT = 60 * 10**9
VMEM_LIMIT = 32 * 1024 * 1024
WHOLE = 60 * 1024 * 1024

SMEM = pl.BlockSpec(memory_space=pltpu.SMEM)
VMEM = pl.BlockSpec(memory_space=pltpu.VMEM)
ANY = pl.BlockSpec(memory_space=pl.ANY)


def dot(a, b):
    return jnp.dot(a, b, preferred_element_type=F32)


def call(kernel, out_shape, in_specs, out_specs, flops=0, bytes_accessed=1 << 20, vmem=VMEM_LIMIT, **more):
    return pl.pallas_call(
        kernel,
        out_shape=out_shape,
        in_specs=in_specs,
        out_specs=out_specs,
        compiler_params=pltpu.CompilerParams(vmem_limit_bytes=vmem),
        cost_estimate=pl.CostEstimate(flops=flops, bytes_accessed=bytes_accessed, transcendentals=0),
        **more,
    )


def swap_cores(a):
    return lax.ppermute(a, "core", [(0, 1), (1, 0)])


def block_copies(to, gate, up, down, out, sems):
    group = out.shape[1]
    first = pl.multiple_of(to * group, group)
    copies = [
        pltpu.make_async_copy(gate.at[pl.ds(first, group)], out.at[0], sems.at[0]),
        pltpu.make_async_copy(up.at[pl.ds(first, group)], out.at[1], sems.at[1]),
    ]
    for j in range(group // HS):
        column = pl.multiple_of(first + j * HS, HS)
        copies.append(
            pltpu.make_async_copy(
                down.at[:, pl.ds(column, HS)], out.at[2, pl.ds(j * HS, HS)], sems.at[2 + j]
            )
        )
    return copies


def expert_at(place):
    return (place // NZ + X0) % NX * NZ + (place % NZ + Z0) % NZ


def exchange(rows):
    order = [expert_at(place) for place in range(rows.shape[0])]
    return lax.all_to_all(rows, E, 0, 0, axis_index_groups=[order], tiled=True)


def exchange_y(blocks, y0):
    order = [(place + y0) % NY for place in range(NY)]
    return lax.all_to_all(blocks, "y", 0, 0, axis_index_groups=[order], tiled=True)


def place_y(y, d, y0):
    return lax.rem(y + 2 * NY - d - y0, NY)


def spread(values, rows):
    slots, experts = values.shape
    lane = lax.broadcasted_iota(jnp.int32, (experts, rows), 1)
    expert = lax.broadcasted_iota(jnp.int32, (experts, rows), 0)
    wide = dot(values.astype(BF), (expert_at(lane // slots) == expert).astype(BF))
    lane = lax.broadcasted_iota(jnp.int32, (slots, rows), 1)
    slot = lax.broadcasted_iota(jnp.int32, (slots, rows), 0)
    return jnp.sum(jnp.where(lane % slots == slot, wide, 0.0), axis=0, keepdims=True)


def position():
    return lax.axis_index("y"), lax.axis_index("core")


def start_kernel(far, slots_ref, tokens, gate, up, down, picked, block, slots, own, rows_out, held, sems, own_sems, out_sems):
    y, c = position()
    width = own.shape[1]
    local_tokens = tokens.shape[0]
    first = pl.multiple_of((y * 2 + c) * width, width)
    fetch_slots = pltpu.make_async_copy(slots_ref, slots, own_sems.at[0])
    fetch = pltpu.make_async_copy(tokens.at[:, pl.ds(first, width)], own, own_sems.at[1])
    fetch_slots.start()
    fetch.start()
    copies = block_copies(lax.rem(y + far, NY), gate, up, down, held, sems)
    for copy in copies:
        copy.start()
    rows = picked.shape[0]
    token = lax.broadcasted_iota(jnp.int32, (local_tokens, rows), 0).astype(F32)
    fetch_slots.wait()
    names = spread(slots[...].astype(F32), rows)
    hit = (names == token).astype(BF)
    for copy in copies:
        copy.wait()
    sends = [pltpu.make_async_copy(held, block, out_sems.at[4])]
    sends[0].start()
    fetch.wait()
    step = rows // 4
    for n in range(4):
        part = pl.ds(n * step, step)
        rows_out[part] = lax.dot_general(
            hit[:, n * step : (n + 1) * step], own[...], (((0,), (0,)), ((), ())), preferred_element_type=F32
        ).astype(BF)
        sends.append(pltpu.make_async_copy(rows_out.at[part], picked.at[part], out_sems.at[n]))
        sends[-1].start()
    for send in sends:
        send.wait()


def start(far, slots, tokens, gate, up, down):
    group = gate.shape[0] // NY
    width = tokens.shape[1] // (2 * NY)
    rows = slots.shape[0] * slots.shape[1]
    return call(
        functools.partial(start_kernel, far),
        (jax.ShapeDtypeStruct((rows, width), BF), jax.ShapeDtypeStruct((3, group, HS), BF)),
        [ANY] * 5,
        (ANY, ANY),
        bytes_accessed=5 << 20,
        vmem=WHOLE,
        scratch_shapes=[
            pltpu.VMEM(slots.shape, jnp.int32),
            pltpu.VMEM((tokens.shape[0], width), BF),
            pltpu.VMEM((rows, width), BF),
            pltpu.VMEM((3, group, HS), BF),
            pltpu.SemaphoreType.DMA((2 + group // HS,)),
            pltpu.SemaphoreType.DMA((2,)),
            pltpu.SemaphoreType.DMA((5,)),
        ],
    )(slots, tokens, gate, up, down)


def pack_kernel(d, gate, up, down, out, sems):
    copies = block_copies(lax.rem(position()[0] + d, NY), gate, up, down, out, sems)
    for copy in copies:
        copy.start()
    for copy in copies:
        copy.wait()


def pack(d, gate, up, down):
    group = gate.shape[0] // NY
    return call(
        functools.partial(pack_kernel, d),
        jax.ShapeDtypeStruct((3, group, HS), BF),
        [ANY, ANY, ANY],
        VMEM,
        vmem=WHOLE,
        scratch_shapes=[pltpu.SemaphoreType.DMA((2 + group // HS,))],
    )(gate, up, down)


def pack_two_kernel(distances, gate, up, down, first, second, held, sems, out_sems):
    y = position()[0]
    copies = [
        block_copies(lax.rem(y + d, NY), gate, up, down, held.at[n], sems.at[n])
        for n, d in enumerate(distances)
    ]
    for block in copies:
        for copy in block:
            copy.start()
    sends = []
    for n, out in enumerate((first, second)):
        for copy in copies[n]:
            copy.wait()
        sends.append(pltpu.make_async_copy(held.at[n], out, out_sems.at[n]))
        sends[-1].start()
    for send in sends:
        send.wait()


def pack_two(distances, gate, up, down):
    group = gate.shape[0] // NY
    block = jax.ShapeDtypeStruct((3, group, HS), BF)
    return call(
        functools.partial(pack_two_kernel, distances),
        (block, block),
        [ANY, ANY, ANY],
        (ANY, ANY),
        vmem=WHOLE,
        scratch_shapes=[
            pltpu.VMEM((2, 3, group, HS), BF),
            pltpu.SemaphoreType.DMA((2, 2 + group // HS)),
            pltpu.SemaphoreType.DMA((2,)),
        ],
    )(gate, up, down)


def ready_kernel(first, second, out, sem):
    copy = pltpu.make_async_copy(first.at[0, pl.ds(0, out.shape[0])], out, sem)
    copy.start()
    copy.wait()


def ready(first, second):
    return call(
        ready_kernel,
        jax.ShapeDtypeStruct((16, HS), BF),
        [ANY, ANY],
        VMEM,
        flops=HINT,
        scratch_shapes=[pltpu.SemaphoreType.DMA],
    )(first, second)


def half_kernel(rows, w0, w1, w2, w3, early, out):
    y, c = position()
    width = rows.shape[1]
    step = 256
    part = pl.ds(pl.multiple_of(c * width, width), width)
    for d, w in enumerate((w0, w1, w2, w3)):
        owner = place_y(y, d, Y_SUMS)
        a = jnp.concatenate([w[0, part], w[1, part]], axis=1)
        for r in range(0, rows.shape[0], step):
            at = pl.ds(r, step)
            out[owner, at] = dot(rows[at], a)


def whole_kernel(rows, w0, w1, w2, w3, half, out):
    y, c = position()
    width = rows.shape[1]
    step = 256
    part = pl.ds(pl.multiple_of((1 - c) * width, width), width)
    for d, w in enumerate((w0, w1, w2, w3)):
        owner = place_y(y, d, Y_SUMS)
        a = jnp.concatenate([w[0, part], w[1, part]], axis=1)
        for r in range(0, rows.shape[0], step):
            at = pl.ds(r, step)
            out[owner, at] = (half[owner, at] + dot(rows[at], a)).astype(BF)


def partial_sums(own, other, blocks, early):
    rows, width = own.shape
    shape = (NY, rows, 2 * HS)
    flops = 2 * rows * width * NY * 2 * HS
    half = call(
        half_kernel, jax.ShapeDtypeStruct(shape, F32), [VMEM] * 5 + [ANY], VMEM, flops=flops
    )(own, *blocks, early)
    return call(whole_kernel, jax.ShapeDtypeStruct(shape, BF), [VMEM] * 6, VMEM, flops=flops)(
        other, *blocks, half
    )


def hidden_kernel(sums, out):
    total = sums[0].astype(F32)
    for k in range(1, NY):
        total = total + sums[k].astype(F32)
    gate, up = total[:, :HS], total[:, HS:]
    hidden = (gate / (1.0 + jnp.exp(-gate)) * up).astype(BF)
    for k in range(NY):
        out[k] = hidden


def hidden_copies(sums):
    return call(
        hidden_kernel, jax.ShapeDtypeStruct((NY, sums.shape[1], HS), BF), [VMEM], VMEM
    )(sums)


def out_kernel(mine, hidden, w0, w1, w2, w3, out):
    y, c = position()
    rows = hidden.shape[1]
    width = out.shape[1]
    first = (c if mine else 1 - c) * width
    owners = [place_y(y, d, Y_HIDDEN) for d in range(NY)]
    a = jnp.concatenate([hidden[k] for k in owners], axis=1)
    for j in range(0, width, 2 * HS):
        one = pl.multiple_of(first + j, HS)
        two = pl.multiple_of(first + j + HS, HS)
        b = jnp.concatenate(
            [
                jnp.concatenate([w[2, pl.ds(one, HS)], w[2, pl.ds(two, HS)]], axis=1)
                for w in (w0, w1, w2, w3)
            ],
            axis=0,
        )
        out[:, pl.ds(j, 2 * HS)] = dot(a, b).astype(out.dtype)


def out_sums(hidden, blocks, width, mine):
    rows = hidden.shape[1]
    return call(
        functools.partial(out_kernel, mine),
        jax.ShapeDtypeStruct((rows, width), F32 if mine else BF),
        [VMEM] * 5,
        VMEM,
        flops=2 * rows * width * NY * HS,
    )(hidden, *blocks)


def result_kernel(keep, given, out, sums, sems):
    rows = keep.shape[0]
    step = rows // 4
    sends = []
    for n in range(4):
        part = pl.ds(n * step, step)
        sums[part] = (keep[part] + given[part].astype(F32)).astype(BF)
        sends.append(pltpu.make_async_copy(sums.at[part], out.at[part], sems.at[n]))
        sends[-1].start()
    for send in sends:
        send.wait()


def result_rows(keep, given):
    return call(
        result_kernel,
        jax.ShapeDtypeStruct(given.shape, BF),
        [VMEM, VMEM],
        ANY,
        scratch_shapes=[pltpu.VMEM(given.shape, BF), pltpu.SemaphoreType.DMA((4,))],
    )(keep, given)


def weight_kernel(slots, gates, counts, out):
    tokens, rows = out.shape[1:]
    names = spread(slots[...].astype(F32), rows)
    hit = names == lax.broadcasted_iota(jnp.int32, (tokens, rows), 0).astype(F32)
    left = gates[...]
    gate = jnp.zeros((1, rows), F32)
    for p in range(3):
        piece = left.astype(BF).astype(F32)
        left = left - piece
        gate = gate + spread(piece, rows)
    left = jnp.where(hit, gate, 0.0) / jnp.maximum(counts[...].astype(F32), 1.0)
    high = left.astype(BF)
    out[0] = high
    out[1] = (left - high.astype(F32)).astype(BF)


def token_weights(slots, gates, counts):
    rows = slots.shape[0] * slots.shape[1]
    return call(
        weight_kernel, jax.ShapeDtypeStruct((2, counts.shape[0], rows), BF), [VMEM] * 3, VMEM
    )(slots, gates, counts)


def finish_kernel(weights, returned, out, held, sems):
    tokens, width = held.shape
    step = width // 2
    high, low = weights[0], weights[1]
    sends = []
    for n in range(2):
        part = pl.ds(n * step, step)
        rows = returned[:, part]
        held[:, part] = (dot(low, rows) + dot(high, rows)).astype(BF)
        sends.append(pltpu.make_async_copy(held.at[:, part], out.at[:, part], sems.at[n]))
        sends[-1].start()
    for send in sends:
        send.wait()


def finish(weights, returned):
    shape = (weights.shape[1], returned.shape[1])
    return call(
        finish_kernel,
        jax.ShapeDtypeStruct(shape, BF),
        [VMEM] * 2,
        ANY,
        scratch_shapes=[pltpu.VMEM(shape, BF), pltpu.SemaphoreType.DMA((2,))],
    )(weights, returned)


def local(tokens, slot_lists, slot_gates, counts, gate_weight, up_weight, down_weight):
    width = tokens.shape[1] // (2 * NY)
    experts, _, slots = slot_lists.shape
    rows = experts * slots
    weights = gate_weight[0], up_weight[0], down_weight[0]
    names = slot_lists.transpose(2, 1, 0).reshape(slots, experts)
    gates = slot_gates.transpose(2, 1, 0).reshape(slots, experts)

    far = 2
    picked, first = start(far, names, tokens, *weights)
    near, back = pack_two((1, 3), *weights)
    blocks = [pack(0, *weights)]
    for d, block in ((1, near), (2, first), (3, back)):
        blocks.append(lax.ppermute(block, "y", [(j, (j + d) % NY) for j in range(NY)]))
    arrived = exchange(picked.reshape(-1, 8, width)).reshape(rows, width)
    arrived, early = lax.optimization_barrier((arrived, ready(blocks[0], blocks[far])))
    other = swap_cores(arrived)
    parts = partial_sums(arrived, other, blocks, early)
    sums = exchange_y(parts, Y_SUMS)
    hidden = exchange_y(hidden_copies(sums), Y_HIDDEN)
    give = swap_cores(out_sums(hidden, blocks, width, False))
    keep = out_sums(hidden, blocks, width, True)
    result = result_rows(keep, give)
    returned = exchange(result.reshape(-1, 8, width))
    return finish(token_weights(names, gates, counts.reshape(-1, 1)), returned.reshape(rows, width))


def solution(mesh):
    fine = Mesh(np.asarray(mesh.devices).reshape(NX * NZ, NY, 2), (E, "y", "core"))
    return jax.shard_map(
        local,
        mesh=fine,
        in_specs=(
            P(E, None),
            P(None, E, None),
            P(None, E, None),
            P(E),
            P(E, None, S),
            P(E, None, S),
            P(E, S, None),
        ),
        out_specs=P(E, S),
        check_vma=False,
    )
```

```python
import functools

import jax
import jax.numpy as jnp
import numpy as np
from jax import lax
from jax.experimental import pallas as pl
from jax.experimental.pallas import tpu as pltpu
from jax.sharding import Mesh, PartitionSpec as P

E = "expert"
NX, NZ = 4, 16
X0, Z0, Y_SUMS, Y_HIDDEN = 0, 11, 3, 2
S = ("y", "core")
NY = 4
HS = 128
BF = jnp.bfloat16
F32 = jnp.float32
HINT = 60 * 10**9
VMEM_LIMIT = 32 * 1024 * 1024
WHOLE = 60 * 1024 * 1024

SMEM = pl.BlockSpec(memory_space=pltpu.SMEM)
VMEM = pl.BlockSpec(memory_space=pltpu.VMEM)
ANY = pl.BlockSpec(memory_space=pl.ANY)


def dot(a, b):
    return jnp.dot(a, b, preferred_element_type=F32)


def call(kernel, out_shape, in_specs, out_specs, flops=0, bytes_accessed=1 << 20, vmem=VMEM_LIMIT, **more):
    return pl.pallas_call(
        kernel,
        out_shape=out_shape,
        in_specs=in_specs,
        out_specs=out_specs,
        compiler_params=pltpu.CompilerParams(vmem_limit_bytes=vmem),
        cost_estimate=pl.CostEstimate(flops=flops, bytes_accessed=bytes_accessed, transcendentals=0),
        **more,
    )


def swap_cores(a):
    return lax.ppermute(a, "core", [(0, 1), (1, 0)])


def block_copies(to, gate, up, down, out, sems):
    group = out.shape[1]
    first = pl.multiple_of(to * group, group)
    copies = [
        pltpu.make_async_copy(gate.at[pl.ds(first, group)], out.at[0], sems.at[0]),
        pltpu.make_async_copy(up.at[pl.ds(first, group)], out.at[1], sems.at[1]),
    ]
    for j in range(group // HS):
        column = pl.multiple_of(first + j * HS, HS)
        copies.append(
            pltpu.make_async_copy(
                down.at[:, pl.ds(column, HS)], out.at[2, pl.ds(j * HS, HS)], sems.at[2 + j]
            )
        )
    return copies


def expert_at(place):
    return (place // NZ + X0) % NX * NZ + (place % NZ + Z0) % NZ


def exchange(rows):
    order = [expert_at(place) for place in range(rows.shape[0])]
    return lax.all_to_all(rows, E, 0, 0, axis_index_groups=[order], tiled=True)


def exchange_y(blocks, y0):
    order = [(place + y0) % NY for place in range(NY)]
    return lax.all_to_all(blocks, "y", 0, 0, axis_index_groups=[order], tiled=True)


def place_y(y, d, y0):
    return lax.rem(y + 2 * NY - d - y0, NY)


def spread(values, rows):
    slots, experts = values.shape
    lane = lax.broadcasted_iota(jnp.int32, (experts, rows), 1)
    expert = lax.broadcasted_iota(jnp.int32, (experts, rows), 0)
    wide = dot(values.astype(BF), (expert_at(lane // slots) == expert).astype(BF))
    lane = lax.broadcasted_iota(jnp.int32, (slots, rows), 1)
    slot = lax.broadcasted_iota(jnp.int32, (slots, rows), 0)
    return jnp.sum(jnp.where(lane % slots == slot, wide, 0.0), axis=0, keepdims=True)


def position():
    return lax.axis_index("y"), lax.axis_index("core")


def start_kernel(far, slots_ref, tokens, gate, up, down, picked, block, slots, own, rows_out, held, sems, own_sems, out_sems):
    y, c = position()
    width = own.shape[1]
    local_tokens = tokens.shape[0]
    first = pl.multiple_of((y * 2 + c) * width, width)
    fetch_slots = pltpu.make_async_copy(slots_ref, slots, own_sems.at[0])
    fetch = pltpu.make_async_copy(tokens.at[:, pl.ds(first, width)], own, own_sems.at[1])
    fetch_slots.start()
    fetch.start()
    copies = block_copies(lax.rem(y + far, NY), gate, up, down, held, sems)
    for copy in copies:
        copy.start()
    rows = picked.shape[0]
    token = lax.broadcasted_iota(jnp.int32, (local_tokens, rows), 0).astype(F32)
    fetch_slots.wait()
    names = spread(slots[...].astype(F32), rows)
    hit = (names == token).astype(BF)
    fetch.wait()
    step = rows // 4
    sends = []
    for n in range(4):
        if n == 1:
            for copy in copies:
                copy.wait()
            sends.append(pltpu.make_async_copy(held, block, out_sems.at[4]))
            sends[-1].start()
        part = pl.ds(n * step, step)
        rows_out[part] = lax.dot_general(
            hit[:, n * step : (n + 1) * step], own[...], (((0,), (0,)), ((), ())), preferred_element_type=F32
        ).astype(BF)
        sends.append(pltpu.make_async_copy(rows_out.at[part], picked.at[part], out_sems.at[n]))
        sends[-1].start()
    for send in sends:
        send.wait()


def start(far, slots, tokens, gate, up, down):
    group = gate.shape[0] // NY
    width = tokens.shape[1] // (2 * NY)
    rows = slots.shape[0] * slots.shape[1]
    return call(
        functools.partial(start_kernel, far),
        (jax.ShapeDtypeStruct((rows, width), BF), jax.ShapeDtypeStruct((3, group, HS), BF)),
        [ANY] * 5,
        (ANY, ANY),
        bytes_accessed=5 << 20,
        vmem=WHOLE,
        scratch_shapes=[
            pltpu.VMEM(slots.shape, jnp.int32),
            pltpu.VMEM((tokens.shape[0], width), BF),
            pltpu.VMEM((rows, width), BF),
            pltpu.VMEM((3, group, HS), BF),
            pltpu.SemaphoreType.DMA((2 + group // HS,)),
            pltpu.SemaphoreType.DMA((2,)),
            pltpu.SemaphoreType.DMA((5,)),
        ],
    )(slots, tokens, gate, up, down)


def pack_kernel(d, gate, up, down, out, sems):
    copies = block_copies(lax.rem(position()[0] + d, NY), gate, up, down, out, sems)
    for copy in copies:
        copy.start()
    for copy in copies:
        copy.wait()


def pack(d, gate, up, down):
    group = gate.shape[0] // NY
    return call(
        functools.partial(pack_kernel, d),
        jax.ShapeDtypeStruct((3, group, HS), BF),
        [ANY, ANY, ANY],
        VMEM,
        vmem=WHOLE,
        scratch_shapes=[pltpu.SemaphoreType.DMA((2 + group // HS,))],
    )(gate, up, down)


def pack_two_kernel(distances, gate, up, down, first, second, held, sems, out_sems):
    y = position()[0]
    copies = [
        block_copies(lax.rem(y + d, NY), gate, up, down, held.at[n], sems.at[n])
        for n, d in enumerate(distances)
    ]
    for block in copies:
        for copy in block:
            copy.start()
    sends = []
    for n, out in enumerate((first, second)):
        for copy in copies[n]:
            copy.wait()
        sends.append(pltpu.make_async_copy(held.at[n], out, out_sems.at[n]))
        sends[-1].start()
    for send in sends:
        send.wait()


def pack_two(distances, gate, up, down):
    group = gate.shape[0] // NY
    block = jax.ShapeDtypeStruct((3, group, HS), BF)
    return call(
        functools.partial(pack_two_kernel, distances),
        (block, block),
        [ANY, ANY, ANY],
        (ANY, ANY),
        vmem=WHOLE,
        scratch_shapes=[
            pltpu.VMEM((2, 3, group, HS), BF),
            pltpu.SemaphoreType.DMA((2, 2 + group // HS)),
            pltpu.SemaphoreType.DMA((2,)),
        ],
    )(gate, up, down)


def ready_kernel(first, second, out, sem):
    copy = pltpu.make_async_copy(first.at[0, pl.ds(0, out.shape[0])], out, sem)
    copy.start()
    copy.wait()


def ready(first, second):
    return call(
        ready_kernel,
        jax.ShapeDtypeStruct((16, HS), BF),
        [ANY, ANY],
        VMEM,
        flops=HINT,
        scratch_shapes=[pltpu.SemaphoreType.DMA],
    )(first, second)


def half_kernel(rows, w0, w1, w2, w3, early, out):
    y, c = position()
    width = rows.shape[1]
    step = 256
    part = pl.ds(pl.multiple_of(c * width, width), width)
    for d, w in enumerate((w0, w1, w2, w3)):
        owner = place_y(y, d, Y_SUMS)
        a = jnp.concatenate([w[0, part], w[1, part]], axis=1)
        for r in range(0, rows.shape[0], step):
            at = pl.ds(r, step)
            out[owner, at] = dot(rows[at], a)


def whole_kernel(rows, w0, w1, w2, w3, half, out):
    y, c = position()
    width = rows.shape[1]
    step = 256
    part = pl.ds(pl.multiple_of((1 - c) * width, width), width)
    for d, w in enumerate((w0, w1, w2, w3)):
        owner = place_y(y, d, Y_SUMS)
        a = jnp.concatenate([w[0, part], w[1, part]], axis=1)
        for r in range(0, rows.shape[0], step):
            at = pl.ds(r, step)
            out[owner, at] = (half[owner, at] + dot(rows[at], a)).astype(BF)


def partial_sums(own, other, blocks, early):
    rows, width = own.shape
    shape = (NY, rows, 2 * HS)
    flops = 2 * rows * width * NY * 2 * HS
    half = call(
        half_kernel, jax.ShapeDtypeStruct(shape, F32), [VMEM] * 5 + [ANY], VMEM, flops=flops
    )(own, *blocks, early)
    return call(whole_kernel, jax.ShapeDtypeStruct(shape, BF), [VMEM] * 6, VMEM, flops=flops)(
        other, *blocks, half
    )


def hidden_kernel(sums, out):
    total = sums[0].astype(F32)
    for k in range(1, NY):
        total = total + sums[k].astype(F32)
    gate, up = total[:, :HS], total[:, HS:]
    hidden = (gate / (1.0 + jnp.exp(-gate)) * up).astype(BF)
    for k in range(NY):
        out[k] = hidden


def hidden_copies(sums):
    return call(
        hidden_kernel, jax.ShapeDtypeStruct((NY, sums.shape[1], HS), BF), [VMEM], VMEM
    )(sums)


def out_kernel(mine, hidden, w0, w1, w2, w3, out):
    y, c = position()
    rows = hidden.shape[1]
    width = out.shape[1]
    first = (c if mine else 1 - c) * width
    owners = [place_y(y, d, Y_HIDDEN) for d in range(NY)]
    a = jnp.concatenate([hidden[k] for k in owners], axis=1)
    for j in range(0, width, 2 * HS):
        one = pl.multiple_of(first + j, HS)
        two = pl.multiple_of(first + j + HS, HS)
        b = jnp.concatenate(
            [
                jnp.concatenate([w[2, pl.ds(one, HS)], w[2, pl.ds(two, HS)]], axis=1)
                for w in (w0, w1, w2, w3)
            ],
            axis=0,
        )
        out[:, pl.ds(j, 2 * HS)] = dot(a, b).astype(out.dtype)


def out_sums(hidden, blocks, width, mine):
    rows = hidden.shape[1]
    return call(
        functools.partial(out_kernel, mine),
        jax.ShapeDtypeStruct((rows, width), F32 if mine else BF),
        [VMEM] * 5,
        VMEM,
        flops=2 * rows * width * NY * HS,
    )(hidden, *blocks)


def result_kernel(keep, given, out, sums, sems):
    rows = keep.shape[0]
    step = rows // 4
    sends = []
    for n in range(4):
        part = pl.ds(n * step, step)
        sums[part] = (keep[part] + given[part].astype(F32)).astype(BF)
        sends.append(pltpu.make_async_copy(sums.at[part], out.at[part], sems.at[n]))
        sends[-1].start()
    for send in sends:
        send.wait()


def result_rows(keep, given):
    return call(
        result_kernel,
        jax.ShapeDtypeStruct(given.shape, BF),
        [VMEM, VMEM],
        ANY,
        scratch_shapes=[pltpu.VMEM(given.shape, BF), pltpu.SemaphoreType.DMA((4,))],
    )(keep, given)


def weight_kernel(slots, gates, counts, out):
    tokens, rows = out.shape[1:]
    names = spread(slots[...].astype(F32), rows)
    hit = names == lax.broadcasted_iota(jnp.int32, (tokens, rows), 0).astype(F32)
    left = gates[...]
    gate = jnp.zeros((1, rows), F32)
    for p in range(3):
        piece = left.astype(BF).astype(F32)
        left = left - piece
        gate = gate + spread(piece, rows)
    left = jnp.where(hit, gate, 0.0) / jnp.maximum(counts[...].astype(F32), 1.0)
    high = left.astype(BF)
    out[0] = high
    out[1] = (left - high.astype(F32)).astype(BF)


def token_weights(slots, gates, counts):
    rows = slots.shape[0] * slots.shape[1]
    return call(
        weight_kernel, jax.ShapeDtypeStruct((2, counts.shape[0], rows), BF), [VMEM] * 3, VMEM
    )(slots, gates, counts)


def finish_kernel(weights, returned, out, held, sems):
    tokens, width = held.shape
    step = width // 2
    high, low = weights[0], weights[1]
    sends = []
    for n in range(2):
        part = pl.ds(n * step, step)
        rows = returned[:, part]
        held[:, part] = (dot(low, rows) + dot(high, rows)).astype(BF)
        sends.append(pltpu.make_async_copy(held.at[:, part], out.at[:, part], sems.at[n]))
        sends[-1].start()
    for send in sends:
        send.wait()


def finish(weights, returned):
    shape = (weights.shape[1], returned.shape[1])
    return call(
        finish_kernel,
        jax.ShapeDtypeStruct(shape, BF),
        [VMEM] * 2,
        ANY,
        scratch_shapes=[pltpu.VMEM(shape, BF), pltpu.SemaphoreType.DMA((2,))],
    )(weights, returned)


def local(tokens, slot_lists, slot_gates, counts, gate_weight, up_weight, down_weight):
    width = tokens.shape[1] // (2 * NY)
    experts, _, slots = slot_lists.shape
    rows = experts * slots
    weights = gate_weight[0], up_weight[0], down_weight[0]
    names = slot_lists.transpose(2, 1, 0).reshape(slots, experts)
    gates = slot_gates.transpose(2, 1, 0).reshape(slots, experts)

    far = 2
    picked, first = start(far, names, tokens, *weights)
    near, back = pack_two((1, 3), *weights)
    blocks = [pack(0, *weights)]
    for d, block in ((1, near), (2, first), (3, back)):
        blocks.append(lax.ppermute(block, "y", [(j, (j + d) % NY) for j in range(NY)]))
    arrived = exchange(picked.reshape(-1, 8, width)).reshape(rows, width)
    arrived, early = lax.optimization_barrier((arrived, ready(blocks[0], blocks[far])))
    other = swap_cores(arrived)
    parts = partial_sums(arrived, other, blocks, early)
    sums = exchange_y(parts, Y_SUMS)
    hidden = exchange_y(hidden_copies(sums), Y_HIDDEN)
    give = swap_cores(out_sums(hidden, blocks, width, False))
    keep = out_sums(hidden, blocks, width, True)
    result = result_rows(keep, give)
    returned = exchange(result.reshape(-1, 8, width))
    return finish(token_weights(names, gates, counts.reshape(-1, 1)), returned.reshape(rows, width))


def solution(mesh):
    fine = Mesh(np.asarray(mesh.devices).reshape(NX * NZ, NY, 2), (E, "y", "core"))
    return jax.shard_map(
        local,
        mesh=fine,
        in_specs=(
            P(E, None),
            P(None, E, None),
            P(None, E, None),
            P(E),
            P(E, None, S),
            P(E, None, S),
            P(E, S, None),
        ),
        out_specs=P(E, S),
        check_vma=False,
    )
```
